32 devices in a mesh: dp: 8 (over y, x, core), tensor: 4 (over z).
Axes of the slice: x: 2, y: 2, z: 4, core: 2. Of those that a mesh axis runs over, the one named last changes fastest.
Arguments:
- token_states: bfloat16 [8192, 2048], P('dp', 'tensor'), may hold values from -6 to 6
- norm_gain: bfloat16 [2048], replicated, may hold values from 0.099609375 to 1.8984375
- gate_weight: bfloat16 [2048, 8192], P('dp', 'tensor'), may hold values from -0.125 to 0.125
- up_weight: bfloat16 [2048, 8192], P('dp', 'tensor'), may hold values from -0.125 to 0.125
- down_weight: bfloat16 [8192, 2048], P('tensor', 'dp'), may hold values from -0.0625 to 0.0625
- embed_weight: bfloat16 [2048, 1024], P('tensor'), may hold values from -1 to 1
- text_owner: int32 [128, 1], P('dp'), may hold values from 0 to 7; in each aligned block of 16 rows (0 to 15, 16 to 31, ...) at most 2 rows name the same one
- text_row: int32 [128], P('dp'), may hold values from 0 to 511
- node_cache: bfloat16 [4096, 1024], P('dp', 'tensor'), may hold values from -6 to 6
- tile_index: int32 [32, 6], P('dp'), may hold values from 0 to 7
- tile_live: int32 [32, 6], P('dp'), may hold values 0 or 1
- tile_weight: bfloat16 [32, 6, 128, 128], P('dp'), may hold values from -0.21875 to 0.21875
- self_weight: bfloat16 [1024, 1024], P(None, 'tensor'), may hold values from -0.1875 to 0.1875
- neighbour_weight: bfloat16 [1024, 1024], P(None, 'tensor'), may hold values from -0.1875 to 0.1875
Outputs:
- node_states: bfloat16 [4096, 1024], P('dp', 'tensor')
The draws below stay inside these ranges and needn't reach their ends.
Inputs may be any that keep to these rules, and one draw needn't show every extreme that they name: `text_owner`: among the 16 texts of one index of dp, at most 2 name the same partition.
All inputs are finite; a program needn't handle non-finite values. No bound on the sum of `tile_live` on one device may be relied on, other than what follows from the above.
Results may differ from the reference program's by a relative error of at most 0.0095.
Values may be sent and summed in bfloat16 or wider, within the bound.
A program may use at most 128 MiB of HBM per device.

```python
import math
import jax
import jax.numpy as jnp
import numpy as np
from jax import lax

D = 2048
FF = 8192
H = 1024
LEN = 64
TEXT_DEV = 16
CAP = 2
TILE = 128
TILES_DEV = 4
BT = 2
SLOTS = 6
LAYERS = 2
TEXTS = 128
TOKENS = 8192
NODE_DEV = 512
NODES = 4096
ROW_TILES = 32
HALO = 256
N_DP = 8


def place_ends(array, rng, smallest, top_value):
    longest = array.shape.index(max(array.shape))
    spots = []
    for shift in (0, 1):
        where = [jax.random.randint(jax.random.fold_in(rng, axis), (), 0, length) for axis, length in enumerate(array.shape)]
        where[longest] = (where[longest] + shift) % array.shape[longest]
        spots.append(tuple(where))
    return array.at[spots[0]].set(smallest).at[spots[1]].set(top_value)


def steps_of(own_key, shape, pieces, least, top_value):
    factor_of = 1.0
    for position, shards_of in pieces:
        steps = jax.random.uniform(jax.random.fold_in(jax.random.fold_in(own_key, 6), position), (shards_of,), jnp.float32, least / len(pieces), top_value / len(pieces))
        factor_of = factor_of * jnp.repeat(jnp.exp(steps), shape[position] // shards_of).reshape((-1,) + (1,) * (len(shape) - 1 - position))
    return factor_of


def assign_block(stream_key, own, number, rows, number_of, top, reach, lean):
    order = jax.random.permutation(stream_key, number_of)
    crowded, usual = load_shares(number_of, rows * top, reach, lean, True), load_shares(number_of, rows * top, reach, lean, False)
    places = jnp.arange(number_of)

    def named(sizes, rotation):
        used = int((sizes > 0).sum())
        fixed = max(1, used // 4)
        passed = fixed + (places - fixed + rotation * (used - fixed)) % max(1, number_of - fixed)
        return jnp.zeros((number_of,), jnp.int32).at[order[jnp.where(places < fixed, places, passed)]].set(jnp.asarray(sizes, jnp.int32))

    sizes = jnp.where(number % 4 == 0, named(crowded, number // 4), named(usual, number - number // 4 - 1))
    mixed = jax.random.permutation(jax.random.fold_in(own, 3), number_of)
    giver, receiver = mixed[0:number_of // 2 * 2:2], mixed[1:number_of // 2 * 2:2]
    room = jnp.minimum(sizes[giver] - 1, reach - sizes[receiver]) // 2
    room = jnp.where((giver == order[0]) | (receiver == order[0]) | (sizes[receiver] == 0), 0, jnp.maximum(room, 0))
    passed = jax.random.randint(jax.random.fold_in(own, 4), (number_of // 2,), 0, 1 << 20) % (room + 1)
    sizes = sizes.at[giver].add(-passed).at[receiver].add(passed)
    items = jnp.searchsorted(jnp.cumsum(sizes), jnp.arange(rows * top), side="right").astype(jnp.int32)
    table = items.reshape(top, rows).T
    table = table[jax.random.permutation(jax.random.fold_in(own, 1), rows)]
    rotation = jax.random.randint(jax.random.fold_in(own, 2), (rows, 1), 0, top)
    return jnp.take_along_axis(table, (jnp.arange(top)[None, :] + rotation) % top, axis=1)


def load_shares(number_of, total, bound, slope, full):
    weights = [(1 << 20) // math.isqrt(rank ** slope) + 1 for rank in range(1, number_of + 1)]
    largest = bound if full else min(bound, max(-(-total // number_of), total * weights[0] // sum(weights)))
    least = 1 if total - largest >= number_of - 1 else 0
    counts, surplus = [largest] + [least] * (number_of - 1), total - largest - least * (number_of - 1)
    while surplus > 0:
        free = [i for i in range(1, number_of) if counts[i] < largest] or [i for i in range(1, number_of) if counts[i] < bound]
        whole, remaining = sum([weights[i] for i in free]), surplus
        for i in free:
            more = min(bound - counts[i], max(1, remaining * weights[i] // whole), surplus)
            counts[i] = counts[i] + more
            surplus = surplus - more
    return np.array(counts)


def noise(own_key, extent, deviation, bound, cuts=(), kind=jnp.bfloat16):
    gain = steps_of(own_key, extent, cuts, -0.22, 0.18) if cuts else 1.0
    result = jax.random.normal(own_key, extent, jnp.float32) * deviation * gain
    return jnp.minimum(jnp.maximum(result, -bound), bound).astype(kind)


def setup_inputs(seed: int = 0) -> dict:
    key_of = jax.random.split(jax.random.key(seed), 15)
    token_states = noise(key_of[0], (TOKENS, D), 1.0, 6.0, ((0, 8), (1, 4)))
    norm_gain = jnp.clip(1.0 + 0.18 * jax.random.normal(key_of[1], (D,), jnp.float32), 0.099609375, 1.8984375).astype(jnp.bfloat16)
    gate_weight = noise(key_of[2], (D, FF), D ** -0.5, 0.125, ((0, 8), (1, 4)))
    up_weight = noise(key_of[3], (D, FF), D ** -0.5, 0.125, ((0, 8), (1, 4)))
    down_weight = noise(key_of[4], (FF, D), FF ** -0.5, 0.0625, ((0, 4), (1, 8)))
    embed_weight = noise(key_of[5], (D, H), (D // LEN) ** -0.5, 1.0, ((0, 4),))
    text_owner_keys = jax.random.split(jax.random.fold_in(key_of[6], 1), TEXTS // TEXT_DEV)
    text_owner_turns = jax.random.permutation(jax.random.fold_in(key_of[6], 3), TEXTS // TEXT_DEV)
    text_owner = jax.vmap(lambda own, number: assign_block(jax.random.fold_in(key_of[6], 2), own, number, TEXT_DEV, N_DP, 1, CAP, 2))(text_owner_keys, text_owner_turns).reshape((TEXTS, 1))
    text_row = place_ends(jax.random.randint(key_of[7], (TEXTS,), 0, NODE_DEV), jax.random.fold_in(key_of[7], 1), 0, NODE_DEV - 1).astype(jnp.int32)
    node_cache = noise(key_of[8], (NODES, H), 1.0, 6.0, ((0, 8), (1, 4)))
    tile_index = place_ends(jax.random.randint(key_of[9], (ROW_TILES, SLOTS), 0, TILES_DEV + 2 * BT), jax.random.fold_in(key_of[9], 1), 0, (TILES_DEV + 2 * BT) - 1).astype(jnp.int32)
    tile_live = place_ends((jax.random.randint(key_of[10], (ROW_TILES, SLOTS), 0, 4) < 3).astype(jnp.int32), jax.random.fold_in(key_of[10], 1), 0, 1)
    tile_weight = noise(key_of[11], (ROW_TILES, SLOTS, TILE, TILE), (SLOTS * TILE) ** -0.5, 0.21875, ((0, 8),))
    self_weight = noise(key_of[12], (H, H), H ** -0.5, 0.1875, ((1, 4),))
    neighbour_weight = noise(key_of[13], (H, H), H ** -0.5, 0.1875, ((1, 4),))
    return dict(token_states=token_states, norm_gain=norm_gain, gate_weight=gate_weight, up_weight=up_weight, down_weight=down_weight, embed_weight=embed_weight, text_owner=text_owner, text_row=text_row, node_cache=node_cache, tile_index=tile_index, tile_live=tile_live, tile_weight=tile_weight, self_weight=self_weight, neighbour_weight=neighbour_weight)


eps = 1e-05

def reference(token_states, norm_gain, gate_weight, up_weight, down_weight, embed_weight, text_owner, text_row, node_cache, tile_index, tile_live, tile_weight, self_weight, neighbour_weight):
    wide = token_states.astype(jnp.float32)
    square = lax.optimization_barrier(jnp.mean(wide * wide, axis=1, keepdims=True))
    normed = (wide * lax.rsqrt(square + eps) * norm_gain.astype(jnp.float32)).astype(jnp.bfloat16)
    gate = jnp.dot(normed, gate_weight, preferred_element_type=jnp.float32)
    upward = jnp.dot(normed, up_weight, preferred_element_type=jnp.float32)
    hidden = (jax.nn.silu(gate) * upward).astype(jnp.bfloat16)
    down = jnp.dot(hidden, down_weight, preferred_element_type=jnp.float32)
    pooled = lax.optimization_barrier(jnp.mean((wide + down).reshape(-1, LEN, D), axis=1))
    fresh = jnp.dot(pooled, embed_weight.astype(jnp.float32), precision=lax.Precision.HIGHEST).astype(jnp.bfloat16)
    target = (text_owner[:, 0] * NODE_DEV + text_row).astype(jnp.int32)
    states = node_cache.astype(jnp.float32).at[target].add(fresh.astype(jnp.float32)).astype(jnp.bfloat16)
    start = (jnp.arange(ROW_TILES) // TILES_DEV * TILES_DEV).astype(jnp.int32)
    where = start[:, None] + tile_index.astype(jnp.int32)
    weights = tile_weight.astype(jnp.float32) * tile_live.astype(jnp.float32)[:, :, None, None]
    near_map = neighbour_weight.astype(jnp.float32)
    for layer in range(LAYERS):
        padded = jnp.pad(states, ((HALO, HALO), (0, 0)))
        tiles = padded.reshape(-1, TILE, H)
        picked = tiles[where].astype(jnp.float32)
        mixed = jnp.einsum('rkij,rkjh->rih', weights, picked, precision=lax.Precision.HIGHEST).reshape(NODES, H)
        total = jnp.dot(states, self_weight, preferred_element_type=jnp.float32) + jnp.dot(mixed, near_map, precision=lax.Precision.HIGHEST)
        states = jax.nn.relu(total).astype(jnp.bfloat16)
    return states
```

```python
import jax
import jax.numpy as jnp
from jax import lax
from jax.sharding import PartitionSpec as P

TILE = 128
BT = 2
LAYERS = 2

eps = 1e-05
f32 = jnp.float32
bf16 = jnp.bfloat16


def exchange(block, axis):
    return lax.all_to_all(block, axis, split_axis=0, concat_axis=0, tiled=True)


def spread(block, axis):
    count = lax.axis_size(axis)
    return exchange(jnp.broadcast_to(block[None], (count,) + block.shape), axis)


def with_halo(block, width):
    count = lax.axis_size("dp")
    forward = [(i, i + 1) for i in range(count - 1)]
    backward = [(target, source) for source, target in forward]
    low = lax.ppermute(block[block.shape[0] - width :], "dp", forward)
    high = lax.ppermute(block[:width], "dp", backward)
    return jnp.concatenate([low, block, high], axis=0)


def side_by_side(blocks):
    return jnp.concatenate([blocks[i] for i in range(blocks.shape[0])], axis=1)


def pooled_hidden(token_states, norm_gain, gate_weight, up_weight, length):
    whole = side_by_side(spread(token_states, "tensor"))
    wide = whole.astype(f32)
    square = jnp.mean(wide * wide, axis=1, keepdims=True)
    normed = (wide * lax.rsqrt(square + eps) * norm_gain.astype(f32)).astype(bf16)
    gate = jnp.dot(
        normed,
        lax.all_gather(gate_weight, "dp", axis=0, tiled=True),
        preferred_element_type=f32,
    )
    upward = jnp.dot(
        normed,
        lax.all_gather(up_weight, "dp", axis=0, tiled=True),
        preferred_element_type=f32,
    )
    hidden = (jax.nn.silu(gate) * upward).astype(bf16)
    return jnp.mean(hidden.astype(f32).reshape(-1, length, hidden.shape[1]), axis=1)


def per_device(
    token_states,
    norm_gain,
    gate_weight,
    up_weight,
    down_weight,
    embed_weight,
    text_owner,
    text_row,
    node_cache,
    tile_index,
    tile_live,
    tile_weight,
    self_weight,
    neighbour_weight,
):
    groups, parts = lax.axis_size("dp"), lax.axis_size("tensor")
    me, col = lax.axis_index("dp"), lax.axis_index("tensor")
    text_count = text_row.shape[0]
    texts = text_count * groups
    length = token_states.shape[0] // text_count
    node_count = node_cache.shape[0]
    halo = BT * TILE

    cache = side_by_side(spread(with_halo(node_cache, halo), "tensor"))
    row_tiles, slots = tile_index.shape
    columns = row_tiles + 2 * BT
    live = (tile_index[:, :, None] == jnp.arange(columns)[None, None, :]) & (
        tile_live[:, :, None] != 0
    )
    adjacency = jnp.zeros((row_tiles, TILE, columns, TILE), f32)
    for slot in range(slots):
        adjacency += jnp.where(
            live[:, slot, None, :, None], tile_weight[:, slot, :, None, :].astype(f32), 0.0
        )
    adjacency = adjacency.astype(bf16).reshape(row_tiles * TILE, columns * TILE)
    place = text_owner[:, 0] * node_count + text_row
    places = spread(place, "dp").reshape(-1)
    width = down_weight.shape[1]
    whole_embed = lax.all_gather(embed_weight, "tensor", axis=0, tiled=True)
    own_embed = lax.dynamic_slice_in_dim(whole_embed, me * width, width, axis=0)
    token_mean = jnp.mean(
        token_states.astype(f32).reshape(text_count, length, -1), axis=1
    )

    mean_hidden = pooled_hidden(token_states, norm_gain, gate_weight, up_weight, length)

    hidden_all = spread(mean_hidden.astype(bf16), "dp").reshape(texts, -1)
    share = jnp.dot(hidden_all, down_weight, preferred_element_type=f32)
    rows = texts // parts
    part = jnp.sum(exchange(share.reshape(parts, rows, width), "tensor"), axis=0)
    pooled = jnp.dot(part, own_embed.astype(f32), precision=lax.Precision.HIGHEST)
    fine = rows // groups
    pooled = jnp.sum(exchange(pooled.reshape(groups, fine, -1), "dp"), axis=0)
    direct = jnp.dot(token_mean, embed_weight.astype(f32), precision=lax.Precision.HIGHEST)
    direct = spread(direct, "dp").reshape(parts, rows, -1)
    direct = jnp.sum(exchange(direct, "tensor"), axis=0)
    direct = lax.dynamic_slice_in_dim(direct, me * fine, fine, axis=0)
    fresh = (pooled + direct).astype(bf16)
    fresh = spread(spread(fresh, "dp").reshape(rows, -1), "tensor").reshape(texts, -1)

    ahead = me * node_count - halo + jnp.arange(cache.shape[0], dtype=jnp.int32)
    hits = (ahead[:, None] == places[None, :]).astype(bf16)
    added = jnp.dot(hits, fresh, preferred_element_type=f32)
    extended = (cache.astype(f32) + added).astype(bf16)
    gathered = extended[halo : halo + node_count]
    for layer in range(LAYERS):
        if layer > 0:
            gathered = side_by_side(spread(states, "tensor"))
            projected = jnp.dot(gathered, neighbour_weight, preferred_element_type=f32)
            projected = with_halo(projected.astype(bf16), halo)
        else:
            projected = jnp.dot(extended, neighbour_weight, preferred_element_type=f32)
            projected = projected.astype(bf16)
        own_part = jnp.dot(gathered, self_weight, preferred_element_type=f32)
        near_part = jnp.dot(adjacency, projected, preferred_element_type=f32)
        states = jax.nn.relu(own_part + near_part).astype(bf16)
    return states


def solution(mesh):
    in_specs = (
        P("dp", "tensor"),
        P(),
        P("dp", "tensor"),
        P("dp", "tensor"),
        P("tensor", "dp"),
        P("tensor", None),
        P("dp", None),
        P("dp"),
        P("dp", "tensor"),
        P("dp", None),
        P("dp", None),
        P("dp", None, None, None),
        P(None, "tensor"),
        P(None, "tensor"),
    )
    out_specs = P("dp", "tensor")
    return jax.shard_map(
        per_device, mesh=mesh, in_specs=in_specs, out_specs=out_specs, check_vma=False
    )
```

```python
import functools

import jax
import jax.numpy as jnp
from jax import lax
from jax.experimental import pallas as pl
from jax.experimental.pallas import tpu as pltpu
from jax.sharding import PartitionSpec as P

TILE = 128
BT = 2
LAYERS = 2

eps = 1e-05
f32 = jnp.float32
bf16 = jnp.bfloat16
MESH = pl.DeviceIdType.MESH


def exchange(block, axis):
    return lax.all_to_all(block, axis, split_axis=0, concat_axis=0, tiled=True)


def spread(block, axis):
    count = lax.axis_size(axis)
    return exchange(jnp.broadcast_to(block[None], (count,) + block.shape), axis)


def with_halo(block, width):
    count = lax.axis_size("dp")
    forward = [(i, i + 1) for i in range(count - 1)]
    backward = [(target, source) for source, target in forward]
    low = lax.ppermute(block[block.shape[0] - width :], "dp", forward)
    high = lax.ppermute(block[:width], "dp", backward)
    return jnp.concatenate([low, block, high], axis=0)


def side_by_side(blocks):
    return jnp.concatenate([blocks[i] for i in range(blocks.shape[0])], axis=1)


def flip(index, bit):
    return index + bit * (1 - 2 * ((index // bit) % 2))


def owner_of(index, mask):
    bit = 1
    while bit <= mask:
        if mask & bit:
            index = flip(index, bit)
        bit *= 2
    return index


def hop_plan(blocks, hops):
    sent, order, turn = {}, [], 0
    while len(sent) < blocks * hops:
        pick = None
        for block in range(blocks):
            for hop in range(hops):
                if (block, hop) in sent or pick is not None:
                    continue
                if hop == 0 or sent.get((block, hop - 1), turn) <= turn - 2:
                    pick = (block, hop)
        if pick is not None:
            sent[pick] = turn
        order.append(pick)
        turn += 1
    return order


def cube_plan(bits, chunks):
    came = {(array, 0, chunk): -2 for array in range(2) for chunk in range(chunks)}
    wanted = {bit: [] for bit in bits}
    for array in range(2):
        span = [0]
        for bit in bits if array == 0 else bits[::-1]:
            for chunk in range(chunks):
                wanted[bit] += [(chunk, len(span), array, mask) for mask in span]
            span = span + [mask ^ bit for mask in span]
    plan = {bit: [] for bit in bits}
    turn = 0
    while any(wanted.values()):
        arrived = []
        for bit in bits:
            ready = [
                item
                for item in sorted(wanted[bit])
                if came.get((item[2], item[3], item[0]), turn) <= turn - 2
            ]
            if ready:
                chunk, _, array, mask = ready[0]
                wanted[bit].remove(ready[0])
                plan[bit].append((array, mask, chunk))
                arrived.append((array, mask ^ bit, chunk))
            else:
                plan[bit].append(None)
        for item in arrived:
            came[item] = turn
        turn += 1
    return plan


def front_kernel(
    groups, parts, chunks, blocks, length, bits, hops, cube,
    tok, gain, gw, uw, out, whole, normed, gfull, ufull,
    hop_send, hop_recv, cube_send, cube_recv, pair_send, pair_recv, own_sem,
):
    me, col = lax.axis_index("dp"), lax.axis_index("tensor")
    depth, width = gw.shape[0], gfull.shape[2]
    rows, local = tok.shape[0] // blocks, tok.shape[1]
    feed, full = (gw, uw), (gfull, ufull)

    barrier = pltpu.get_barrier_semaphore()
    partners = [flip(me, bit) for bit in [1] + bits]
    for partner in partners:
        pl.semaphore_signal(barrier, inc=1, device_id=(partner, col), device_id_type=MESH)

    @pl.when(col > 0)
    def _():
        pl.semaphore_signal(barrier, inc=1, device_id=(me, col - 1), device_id_type=MESH)

    @pl.when(col < parts - 1)
    def _():
        pl.semaphore_signal(barrier, inc=1, device_id=(me, col + 1), device_id_type=MESH)

    own = [pltpu.make_async_copy(tok, whole.at[col], own_sem.at[0])]
    for array in range(2):
        for chunk in range(chunks):
            own.append(
                pltpu.make_async_copy(
                    feed[array].at[:, pl.ds(chunk * width, width)],
                    full[array].at[chunk, pl.ds(pl.multiple_of(me * depth, depth), depth)],
                    own_sem.at[1 + array * chunks + chunk],
                )
            )
    for copy in own:
        copy.start()

    sides = (col + parts - 1) // parts + (2 * parts - 2 - col) // parts
    pl.semaphore_wait(barrier, len(partners) + sides)

    def shard(array, mask, chunk):
        at = pl.multiple_of(owner_of(me, mask) * depth, depth)
        return full[array].at[chunk, pl.ds(at, depth)]

    def swap(array, mask, chunk, bit, send, recv):
        src = shard(array, mask, chunk)
        if mask == 0:
            src = feed[array].at[:, pl.ds(chunk * width, width)]
        return pltpu.make_async_remote_copy(
            src_ref=src,
            dst_ref=shard(array, mask, chunk),
            send_sem=send,
            recv_sem=recv,
            device_id=(flip(me, bit), col),
            device_id_type=MESH,
        )

    def landed(array, mask, chunk, bit, send, recv):
        there = shard(array, mask ^ bit, chunk)
        return pltpu.make_async_remote_copy(
            src_ref=there,
            dst_ref=there,
            send_sem=send,
            recv_sem=recv,
            device_id=(flip(me, bit), col),
            device_id_type=MESH,
        )

    def hop(turn, way, incoming):
        block, far = hops[turn]
        step = 1 if way == 0 else -1
        held = col - step * far
        if incoming:
            held = col - step * (far + 1)
            there = (held >= 0) & (held < parts)
        else:
            there = (held >= 0) & (held < parts) & (col + step >= 0) & (col + step < parts)
        span = pl.ds(block * rows, rows)
        src = whole.at[held, span]
        if not incoming and far == 0:
            src = tok.at[span]
        copy = pltpu.make_async_remote_copy(
            src_ref=src,
            dst_ref=whole.at[held, span],
            send_sem=hop_send.at[way, turn],
            recv_sem=hop_recv.at[way, turn],
            device_id=(me, col + step),
            device_id_type=MESH,
        )
        return there, copy

    def pair(array, mask, chunk):
        at = (array * (groups // 2) + mask // 2) * chunks + chunk
        return array, mask, chunk, 1, pair_send.at[at], pair_recv.at[at]

    def normalise(block):
        def one(part, _):
            span = pl.ds(pl.multiple_of(block * rows + part * length, length), length)
            square = jnp.zeros((length, 1), f32)
            for p in range(parts):
                wide = whole[p, span, :].astype(f32)
                square += jnp.sum(wide * wide, axis=1, keepdims=True)
            scale = lax.rsqrt(square * (1.0 / (parts * local)) + eps)
            for p in range(parts):
                wide = whole[p, span, :].astype(f32)
                normed[span, p * local : (p + 1) * local] = (
                    wide * scale * gain[:, p * local : (p + 1) * local].astype(f32)
                ).astype(bf16)
            return 0

        lax.fori_loop(0, rows // length, one, 0)

    def work(block, chunk):
        x = normed[pl.ds(pl.multiple_of(block * rows, rows), rows), :]
        gate = jnp.dot(x, gfull[chunk], preferred_element_type=f32)
        upward = jnp.dot(x, ufull[chunk], preferred_element_type=f32)
        hidden = (gate / (1.0 + jnp.exp(-gate)) * upward).astype(bf16).astype(f32)
        mean = jnp.sum(hidden.reshape(rows // length, length, width), axis=1)
        out[chunk, block] = mean * (1.0 / length)

    turns = max([len(hops)] + [len(cube[bit]) for bit in bits])
    missing = {chunk: 2 * groups for chunk in range(chunks)}
    unhopped = {block: parts - 1 for block in range(blocks)}
    ready_chunks, ready_blocks = [], []
    flying = []

    for array in range(2):
        for chunk in range(chunks):
            swap(*pair(array, 0, chunk)).start()
            flying.append((array, 0, chunk))
    for turn in range(turns + 3):
        back = turn - 2
        new_blocks, new_chunks = [], []
        settled = flying
        flying = []
        if 0 <= back < turns:
            if back < len(hops) and hops[back] is not None:
                for way in range(2):
                    there, copy = hop(back, way, True)
                    pl.when(there)(copy.wait_recv)
                    there, copy = hop(back, way, False)
                    pl.when(there)(copy.wait_send)
                unhopped[hops[back][0]] -= 1
                if unhopped[hops[back][0]] == 0:
                    new_blocks.append(hops[back][0])
            for n, bit in enumerate(bits):
                item = cube[bit][back] if back < len(cube[bit]) else None
                if item is not None:
                    sems = (cube_send.at[n, back], cube_recv.at[n, back])
                    landed(*item, bit, *sems).wait_recv()
                    swap(*item, bit, *sems).wait_send()
                    moved = (item[0], item[1] ^ bit, item[2])
                    swap(*pair(*moved)).start()
                    flying.append(moved)
        if turn < len(hops) and hops[turn] is not None:
            for way in range(2):
                there, copy = hop(turn, way, False)
                pl.when(there)(copy.start)
        for n, bit in enumerate(bits):
            item = cube[bit][turn] if turn < len(cube[bit]) else None
            if item is not None:
                swap(*item, bit, cube_send.at[n, turn], cube_recv.at[n, turn]).start()
        if turn == 0:
            for copy in own:
                copy.wait()
            for chunk in range(chunks):
                missing[chunk] -= 2
        for block in new_blocks:
            normalise(block)
            if ready_chunks:
                def across(n, _, block=block):
                    work(block, n)
                    return 0
                lax.fori_loop(0, len(ready_chunks), across, 0)
            ready_blocks.append(block)
        for array, mask, chunk in settled:
            landed(*pair(array, mask, chunk)).wait_recv()
            swap(*pair(array, mask, chunk)).wait_send()
            missing[chunk] -= 1
        for array, mask, chunk in settled:
            if mask:
                missing[chunk] -= 1
        for chunk in range(chunks):
            if missing[chunk] == 0 and chunk not in ready_chunks:
                assert chunk == len(ready_chunks)
                if ready_blocks:
                    assert ready_blocks == list(range(len(ready_blocks)))
                    def down(n, _, chunk=chunk):
                        work(n, chunk)
                        return 0
                    lax.fori_loop(0, len(ready_blocks), down, 0)
                ready_chunks.append(chunk)
    assert len(ready_chunks) == chunks and len(ready_blocks) == blocks and not flying


def pooled_hidden(token_states, norm_gain, gate_weight, up_weight, length):
    groups, parts = lax.axis_size("dp"), lax.axis_size("tensor")
    tokens, local = token_states.shape
    depth, hidden = gate_weight.shape
    chunks = blocks = 4
    width, rows = hidden // chunks, tokens // blocks
    bits = [1 << n for n in range(1, (groups - 1).bit_length())]
    hops = hop_plan(blocks, parts - 1)
    cube = cube_plan(bits, chunks)
    turns = max(len(cube[bit]) for bit in bits)
    pairs = 2 * chunks * (groups // 2)
    sem = pltpu.SemaphoreType.DMA
    features = parts * local
    any_space = pl.BlockSpec(memory_space=pl.ANY)
    vmem = pl.BlockSpec(memory_space=pltpu.VMEM)
    mean = pl.pallas_call(
        functools.partial(
            front_kernel, groups, parts, chunks, blocks, length, bits, hops, cube
        ),
        out_shape=jax.ShapeDtypeStruct((chunks, blocks, rows // length, width), f32),
        in_specs=[any_space, vmem, any_space, any_space],
        out_specs=vmem,
        scratch_shapes=[
            pltpu.VMEM((parts, tokens, local), bf16),
            pltpu.VMEM((tokens, features), bf16),
            pltpu.VMEM((chunks, groups * depth, width), bf16),
            pltpu.VMEM((chunks, groups * depth, width), bf16),
            sem((2, len(hops))),
            sem((2, len(hops))),
            sem((len(bits), turns)),
            sem((len(bits), turns)),
            sem((pairs,)),
            sem((pairs,)),
            sem((1 + 2 * chunks,)),
        ],
        compiler_params=pltpu.CompilerParams(
            collective_id=0, has_side_effects=True, vmem_limit_bytes=48 << 20
        ),
        cost_estimate=pl.CostEstimate(
            flops=4 * tokens * features * hidden,
            bytes_accessed=4 * features * hidden,
            transcendentals=tokens * hidden,
        ),
        name="gather_and_pool",
    )(token_states, norm_gain[None], gate_weight, up_weight)
    return jnp.transpose(mean, (1, 2, 0, 3)).reshape(tokens // length, hidden)


def per_device(
    token_states,
    norm_gain,
    gate_weight,
    up_weight,
    down_weight,
    embed_weight,
    text_owner,
    text_row,
    node_cache,
    tile_index,
    tile_live,
    tile_weight,
    self_weight,
    neighbour_weight,
):
    groups, parts = lax.axis_size("dp"), lax.axis_size("tensor")
    me, col = lax.axis_index("dp"), lax.axis_index("tensor")
    text_count = text_row.shape[0]
    texts = text_count * groups
    length = token_states.shape[0] // text_count
    node_count = node_cache.shape[0]
    halo = BT * TILE

    cache = side_by_side(spread(with_halo(node_cache, halo), "tensor"))
    row_tiles, slots = tile_index.shape
    columns = row_tiles + 2 * BT
    live = (tile_index[:, :, None] == jnp.arange(columns)[None, None, :]) & (
        tile_live[:, :, None] != 0
    )
    adjacency = jnp.zeros((row_tiles, TILE, columns, TILE), f32)
    for slot in range(slots):
        adjacency += jnp.where(
            live[:, slot, None, :, None], tile_weight[:, slot, :, None, :].astype(f32), 0.0
        )
    adjacency = adjacency.astype(bf16).reshape(row_tiles * TILE, columns * TILE)
    place = text_owner[:, 0] * node_count + text_row
    places = spread(place, "dp").reshape(-1)
    width = down_weight.shape[1]
    whole_embed = lax.all_gather(embed_weight, "tensor", axis=0, tiled=True)
    own_embed = lax.dynamic_slice_in_dim(whole_embed, me * width, width, axis=0)
    token_mean = jnp.mean(
        token_states.astype(f32).reshape(text_count, length, -1), axis=1
    )

    mean_hidden = pooled_hidden(token_states, norm_gain, gate_weight, up_weight, length)

    hidden_all = spread(mean_hidden.astype(bf16), "dp").reshape(texts, -1)
    share = jnp.dot(hidden_all, down_weight, preferred_element_type=f32)
    rows = texts // parts
    part = jnp.sum(exchange(share.reshape(parts, rows, width), "tensor"), axis=0)
    pooled = jnp.dot(part, own_embed.astype(f32), precision=lax.Precision.HIGHEST)
    fine = rows // groups
    pooled = jnp.sum(exchange(pooled.reshape(groups, fine, -1), "dp"), axis=0)
    direct = jnp.dot(token_mean, embed_weight.astype(f32), precision=lax.Precision.HIGHEST)
    direct = spread(direct, "dp").reshape(parts, rows, -1)
    direct = jnp.sum(exchange(direct, "tensor"), axis=0)
    direct = lax.dynamic_slice_in_dim(direct, me * fine, fine, axis=0)
    fresh = (pooled + direct).astype(bf16)
    fresh = spread(spread(fresh, "dp").reshape(rows, -1), "tensor").reshape(texts, -1)

    ahead = me * node_count - halo + jnp.arange(cache.shape[0], dtype=jnp.int32)
    hits = (ahead[:, None] == places[None, :]).astype(bf16)
    added = jnp.dot(hits, fresh, preferred_element_type=f32)
    extended = (cache.astype(f32) + added).astype(bf16)
    gathered = extended[halo : halo + node_count]
    for layer in range(LAYERS):
        if layer > 0:
            gathered = side_by_side(spread(states, "tensor"))
            projected = jnp.dot(gathered, neighbour_weight, preferred_element_type=f32)
            projected = with_halo(projected.astype(bf16), halo)
        else:
            projected = jnp.dot(extended, neighbour_weight, preferred_element_type=f32)
            projected = projected.astype(bf16)
        own_part = jnp.dot(gathered, self_weight, preferred_element_type=f32)
        near_part = jnp.dot(adjacency, projected, preferred_element_type=f32)
        states = jax.nn.relu(own_part + near_part).astype(bf16)
    return states


def solution(mesh):
    in_specs = (
        P("dp", "tensor"),
        P(),
        P("dp", "tensor"),
        P("dp", "tensor"),
        P("tensor", "dp"),
        P("tensor", None),
        P("dp", None),
        P("dp"),
        P("dp", "tensor"),
        P("dp", None),
        P("dp", None),
        P("dp", None, None, None),
        P(None, "tensor"),
        P(None, "tensor"),
    )
    out_specs = P("dp", "tensor")
    return jax.shard_map(
        per_device, mesh=mesh, in_specs=in_specs, out_specs=out_specs, check_vma=False
    )
```

```python
import functools

import jax
import jax.numpy as jnp
from jax import lax
from jax.experimental import pallas as pl
from jax.experimental.pallas import tpu as pltpu
from jax.sharding import PartitionSpec as P

TILE = 128
BT = 2
LAYERS = 2

eps = 1e-05
f32 = jnp.float32
bf16 = jnp.bfloat16
MESH = pl.DeviceIdType.MESH


def flip(index, bit):
    return index + bit * (1 - 2 * ((index // bit) % 2))


def owner_of(index, mask):
    bit = 1
    while bit <= mask:
        if mask & bit:
            index = flip(index, bit)
        bit *= 2
    return index


def hop_plan(blocks, hops):
    sent, order, turn = {}, [], 0
    while len(sent) < blocks * hops:
        pick = None
        for block in range(blocks):
            for hop in range(hops):
                if (block, hop) in sent or pick is not None:
                    continue
                if hop == 0 or sent.get((block, hop - 1), turn) <= turn - 2:
                    pick = (block, hop)
        if pick is not None:
            sent[pick] = turn
        order.append(pick)
        turn += 1
    return order


def cube_plan(bits, chunks):
    came = {(array, 0, chunk): -2 for array in range(2) for chunk in range(chunks)}
    wanted = {bit: [] for bit in bits}
    for array in range(2):
        span = [0]
        for bit in bits if array == 0 else bits[::-1]:
            for chunk in range(chunks):
                wanted[bit] += [(chunk, len(span), array, mask) for mask in span]
            span = span + [mask ^ bit for mask in span]
    plan = {bit: [] for bit in bits}
    turn = 0
    while any(wanted.values()):
        arrived = []
        for bit in bits:
            ready = [
                item
                for item in sorted(wanted[bit])
                if came.get((item[2], item[3], item[0]), turn) <= turn - 2
            ]
            if ready:
                chunk, _, array, mask = ready[0]
                wanted[bit].remove(ready[0])
                plan[bit].append((array, mask, chunk))
                arrived.append((array, mask ^ bit, chunk))
            else:
                plan[bit].append(None)
        for item in arrived:
            came[item] = turn
        turn += 1
    return plan


def front_kernel(
    groups, parts, chunks, blocks, length, bits, hops, cube,
    tok, gain, gw, uw, out, own_mean, whole, normed, gfull, ufull,
    hop_send, hop_recv, cube_send, cube_recv, pair_send, pair_recv, own_sem,
):
    me, col = lax.axis_index("dp"), lax.axis_index("tensor")
    depth, width = gw.shape[0], gfull.shape[2]
    rows, local = tok.shape[0] // blocks, tok.shape[1]
    feed, full = (gw, uw), (gfull, ufull)

    barrier = pltpu.get_barrier_semaphore()
    partners = [flip(me, bit) for bit in [1] + bits]
    for partner in partners:
        pl.semaphore_signal(barrier, inc=1, device_id=(partner, col), device_id_type=MESH)

    @pl.when(col > 0)
    def _():
        pl.semaphore_signal(barrier, inc=1, device_id=(me, col - 1), device_id_type=MESH)

    @pl.when(col < parts - 1)
    def _():
        pl.semaphore_signal(barrier, inc=1, device_id=(me, col + 1), device_id_type=MESH)

    own = [pltpu.make_async_copy(tok, whole.at[col], own_sem.at[0])]
    for array in range(2):
        for chunk in range(chunks):
            own.append(
                pltpu.make_async_copy(
                    feed[array].at[:, pl.ds(chunk * width, width)],
                    full[array].at[chunk, pl.ds(pl.multiple_of(me * depth, depth), depth)],
                    own_sem.at[1 + array * chunks + chunk],
                )
            )
    for copy in own:
        copy.start()

    sides = (col + parts - 1) // parts + (2 * parts - 2 - col) // parts
    pl.semaphore_wait(barrier, len(partners) + sides)

    def shard(array, mask, chunk):
        at = pl.multiple_of(owner_of(me, mask) * depth, depth)
        return full[array].at[chunk, pl.ds(at, depth)]

    def swap(array, mask, chunk, bit, send, recv):
        src = shard(array, mask, chunk)
        if mask == 0:
            src = feed[array].at[:, pl.ds(chunk * width, width)]
        return pltpu.make_async_remote_copy(
            src_ref=src,
            dst_ref=shard(array, mask, chunk),
            send_sem=send,
            recv_sem=recv,
            device_id=(flip(me, bit), col),
            device_id_type=MESH,
        )

    def landed(array, mask, chunk, bit, send, recv):
        there = shard(array, mask ^ bit, chunk)
        return pltpu.make_async_remote_copy(
            src_ref=there,
            dst_ref=there,
            send_sem=send,
            recv_sem=recv,
            device_id=(flip(me, bit), col),
            device_id_type=MESH,
        )

    def hop(turn, way, incoming):
        block, far = hops[turn]
        step = 1 if way == 0 else -1
        held = col - step * far
        if incoming:
            held = col - step * (far + 1)
            there = (held >= 0) & (held < parts)
        else:
            there = (held >= 0) & (held < parts) & (col + step >= 0) & (col + step < parts)
        span = pl.ds(block * rows, rows)
        src = whole.at[held, span]
        if not incoming and far == 0:
            src = tok.at[span]
        copy = pltpu.make_async_remote_copy(
            src_ref=src,
            dst_ref=whole.at[held, span],
            send_sem=hop_send.at[way, turn],
            recv_sem=hop_recv.at[way, turn],
            device_id=(me, col + step),
            device_id_type=MESH,
        )
        return there, copy

    def pair(array, mask, chunk):
        at = (array * (groups // 2) + mask // 2) * chunks + chunk
        return array, mask, chunk, 1, pair_send.at[at], pair_recv.at[at]

    def normalise(block):
        def one(part, _):
            span = pl.ds(pl.multiple_of(block * rows + part * length, length), length)
            square = jnp.zeros((length, 1), f32)
            for p in range(parts):
                wide = whole[p, span, :].astype(f32)
                square += jnp.sum(wide * wide, axis=1, keepdims=True)
            scale = lax.rsqrt(square * (1.0 / (parts * local)) + eps)
            for p in range(parts):
                wide = whole[p, span, :].astype(f32)
                normed[span, p * local : (p + 1) * local] = (
                    wide * scale * gain[:, p * local : (p + 1) * local].astype(f32)
                ).astype(bf16)
            return 0

        lax.fori_loop(0, rows // length, one, 0)

    def work(block, chunk):
        x = normed[pl.ds(pl.multiple_of(block * rows, rows), rows), :]
        gate = jnp.dot(x, gfull[chunk], preferred_element_type=f32)
        upward = jnp.dot(x, ufull[chunk], preferred_element_type=f32)
        hidden = (gate / (1.0 + jnp.exp(-gate)) * upward).astype(bf16).astype(f32)
        mean = jnp.sum(hidden.reshape(rows // length, length, width), axis=1)
        out[chunk, block] = mean * (1.0 / length)

    turns = max([len(hops)] + [len(cube[bit]) for bit in bits])
    missing = {chunk: 2 * groups for chunk in range(chunks)}
    unhopped = {block: parts - 1 for block in range(blocks)}
    ready_chunks, ready_blocks = [], []
    flying = []

    for array in range(2):
        for chunk in range(chunks):
            swap(*pair(array, 0, chunk)).start()
            flying.append((array, 0, chunk))
    for turn in range(turns + 3):
        back = turn - 2
        new_blocks, new_chunks = [], []
        settled = flying
        flying = []
        if 0 <= back < turns:
            if back < len(hops) and hops[back] is not None:
                for way in range(2):
                    there, copy = hop(back, way, True)
                    pl.when(there)(copy.wait_recv)
                    there, copy = hop(back, way, False)
                    pl.when(there)(copy.wait_send)
                unhopped[hops[back][0]] -= 1
                if unhopped[hops[back][0]] == 0:
                    new_blocks.append(hops[back][0])
            for n, bit in enumerate(bits):
                item = cube[bit][back] if back < len(cube[bit]) else None
                if item is not None:
                    sems = (cube_send.at[n, back], cube_recv.at[n, back])
                    landed(*item, bit, *sems).wait_recv()
                    swap(*item, bit, *sems).wait_send()
                    moved = (item[0], item[1] ^ bit, item[2])
                    swap(*pair(*moved)).start()
                    flying.append(moved)
        if turn < len(hops) and hops[turn] is not None:
            for way in range(2):
                there, copy = hop(turn, way, False)
                pl.when(there)(copy.start)
        for n, bit in enumerate(bits):
            item = cube[bit][turn] if turn < len(cube[bit]) else None
            if item is not None:
                swap(*item, bit, cube_send.at[n, turn], cube_recv.at[n, turn]).start()
        if turn == 0:
            for copy in own:
                copy.wait()

            def average(text, _):
                span = pl.ds(pl.multiple_of(text * length, length), length)
                own_mean[text] = jnp.sum(
                    whole[col, span, :].astype(f32), axis=0, keepdims=True
                ) * (1.0 / length)
                return 0

            lax.fori_loop(0, tok.shape[0] // length, average, 0)
            for chunk in range(chunks):
                missing[chunk] -= 2
        for block in new_blocks:
            normalise(block)
            if ready_chunks:
                def across(n, _, block=block):
                    work(block, n)
                    return 0
                lax.fori_loop(0, len(ready_chunks), across, 0)
            ready_blocks.append(block)
        for array, mask, chunk in settled:
            landed(*pair(array, mask, chunk)).wait_recv()
            swap(*pair(array, mask, chunk)).wait_send()
            missing[chunk] -= 1
        for array, mask, chunk in settled:
            if mask:
                missing[chunk] -= 1
        for chunk in range(chunks):
            if missing[chunk] == 0 and chunk not in ready_chunks:
                assert chunk == len(ready_chunks)
                if ready_blocks:
                    assert ready_blocks == list(range(len(ready_blocks)))
                    def down(n, _, chunk=chunk):
                        work(n, chunk)
                        return 0
                    lax.fori_loop(0, len(ready_blocks), down, 0)
                ready_chunks.append(chunk)
    assert len(ready_chunks) == chunks and len(ready_blocks) == blocks and not flying


def pooled_hidden(token_states, norm_gain, gate_weight, up_weight, length):
    groups, parts = lax.axis_size("dp"), lax.axis_size("tensor")
    tokens, local = token_states.shape
    depth, hidden = gate_weight.shape
    chunks = blocks = 4
    width, rows = hidden // chunks, tokens // blocks
    bits = [1 << n for n in range(1, (groups - 1).bit_length())]
    hops = hop_plan(blocks, parts - 1)
    cube = cube_plan(bits, chunks)
    turns = max(len(cube[bit]) for bit in bits)
    pairs = 2 * chunks * (groups // 2)
    sem = pltpu.SemaphoreType.DMA
    features = parts * local
    any_space = pl.BlockSpec(memory_space=pl.ANY)
    vmem = pl.BlockSpec(memory_space=pltpu.VMEM)
    mean, own_mean = pl.pallas_call(
        functools.partial(
            front_kernel, groups, parts, chunks, blocks, length, bits, hops, cube
        ),
        out_shape=[
            jax.ShapeDtypeStruct((chunks, blocks, rows // length, width), f32),
            jax.ShapeDtypeStruct((tokens // length, 1, local), f32),
        ],
        in_specs=[any_space, vmem, any_space, any_space],
        out_specs=[vmem, vmem],
        scratch_shapes=[
            pltpu.VMEM((parts, tokens, local), bf16),
            pltpu.VMEM((tokens, features), bf16),
            pltpu.VMEM((chunks, groups * depth, width), bf16),
            pltpu.VMEM((chunks, groups * depth, width), bf16),
            sem((2, len(hops))),
            sem((2, len(hops))),
            sem((len(bits), turns)),
            sem((len(bits), turns)),
            sem((pairs,)),
            sem((pairs,)),
            sem((1 + 2 * chunks,)),
        ],
        compiler_params=pltpu.CompilerParams(
            collective_id=0, has_side_effects=True, vmem_limit_bytes=48 << 20
        ),
        cost_estimate=pl.CostEstimate(
            flops=4 * tokens * features * hidden,
            bytes_accessed=4 * features * hidden,
            transcendentals=tokens * hidden,
        ),
        name="gather_and_pool",
    )(token_states, norm_gain[None], gate_weight, up_weight)
    mean = jnp.transpose(mean, (1, 2, 0, 3)).reshape(tokens // length, hidden)
    return mean, own_mean[:, 0]


def line_copies(buffer, col, parts, me, cuts, send, recv):
    size = buffer.shape[1] // cuts

    def copy(way, far, cut, incoming):
        step = 1 if way == 0 else -1
        held = col - step * (far + 1 if incoming else far)
        there = (held >= 0) & (held < parts)
        if not incoming:
            there = there & (col + step >= 0) & (col + step < parts)
        part = buffer.at[held, pl.ds(cut * size, size)]
        return there, pltpu.make_async_remote_copy(
            src_ref=part,
            dst_ref=part,
            send_sem=send.at[way, far, cut],
            recv_sem=recv.at[way, far, cut],
            device_id=(me, col + step),
            device_id_type=MESH,
        )

    def advance(far):
        for cut in range(cuts):
            for way in range(2):
                if far > 0:
                    there, came = copy(way, far - 1, cut, True)
                    pl.when(there)(came.wait_recv)
                if far < parts - 1:
                    there, gone = copy(way, far, cut, False)
                    pl.when(there)(gone.start)

    def finish():
        for far in range(parts - 1):
            for cut in range(cuts):
                for way in range(2):
                    there, gone = copy(way, far, cut, False)
                    pl.when(there)(gone.wait_send)

    return advance, finish


def tail_kernel(
    groups, parts, layers, cuts,
    mean, token_mean, down, embed, place, cache, adjacency, self_w, near_w, out,
    hidden, spots, share, pooled, terms, sums, fresh, states, nodes, extended,
    a_send, a_recv, p_send, p_recv, b_send, b_recv, c_send, c_recv,
    d_send, d_recv, e_send, e_recv, line_send, line_recv, halo_send, halo_recv,
):
    me, col = lax.axis_index("dp"), lax.axis_index("tensor")
    texts, width = mean.shape[0], down.shape[1]
    count, local = cache.shape
    halo = (extended.shape[1] - count) // 2
    split = groups // parts

    barrier = pltpu.get_barrier_semaphore()
    for s in range(1, groups):
        pl.semaphore_signal(
            barrier, inc=1, device_id=((me + s) % groups, col), device_id_type=MESH
        )
    for s in range(1, parts):
        pl.semaphore_signal(
            barrier, inc=1, device_id=(me, (col + s) % parts), device_id_type=MESH
        )
    hidden[me] = mean[...].astype(bf16)
    spots[me] = place[...]
    nodes[0, col] = cache[...]
    pl.semaphore_wait(barrier, groups + parts - 2)

    def along(axis, src, dst, send, recv):
        size = groups if axis == 0 else parts
        mine = me if axis == 0 else col

        def copy(s, incoming):
            peer = (mine + s) % size
            slot = dst(mine)
            if incoming:
                slot = dst((mine + size - s) % size)
            return pltpu.make_async_remote_copy(
                src_ref=slot if incoming else src(peer),
                dst_ref=slot,
                send_sem=send.at[s],
                recv_sem=recv.at[s],
                device_id=(peer, col) if axis == 0 else (me, peer),
                device_id_type=MESH,
            )

        def start():
            for s in range(1, size):
                copy(s, False).start()

        def wait():
            for s in range(1, size):
                copy(s, True).wait_recv()
            for s in range(1, size):
                copy(s, False).wait_send()

        return start, wait

    advance, finish = line_copies(
        nodes.at[0], col, parts, me, cuts, line_send.at[0], line_recv.at[0]
    )
    start_a, wait_a = along(0, lambda p: hidden.at[me], lambda p: hidden.at[p], a_send, a_recv)
    start_p, wait_p = along(0, lambda p: spots.at[me], lambda p: spots.at[p], p_send, p_recv)
    start_a()
    start_p()
    advance(0)
    wait_a()
    wait_p()
    advance(1)
    part = jnp.dot(
        hidden[...].reshape(groups * texts, hidden.shape[2]),
        down[...],
        preferred_element_type=f32,
    )
    share[...] = part.reshape(groups, texts, width)
    pooled[me] = share[me]
    start, wait = along(0, lambda p: share.at[p], lambda p: pooled.at[p], b_send, b_recv)
    start()
    wait()
    terms[col] = pooled[pl.ds(col * split, split)]
    start, wait = along(
        1, lambda p: pooled.at[pl.ds(p * split, split)], lambda p: terms.at[p], c_send, c_recv
    )
    start()
    if parts > 2:
        advance(2)
    wait()
    total = jnp.zeros((texts, embed.shape[1]), f32)
    for i in range(split):
        value = token_mean[:, i * width : (i + 1) * width]
        for p in range(parts):
            value += terms[p, i]
        high = value.astype(bf16)
        low = (value - high.astype(f32)).astype(bf16)
        rows = embed[i * width : (i + 1) * width, :]
        total += jnp.dot(high, rows, preferred_element_type=f32)
        total += jnp.dot(low, rows, preferred_element_type=f32)
    sums[col] = total.astype(bf16)
    start, wait = along(1, lambda p: sums.at[col], lambda p: sums.at[p], d_send, d_recv)
    start()
    wait()
    total = jnp.zeros((texts, embed.shape[1]), f32)
    for p in range(parts):
        total += sums[p].astype(f32)
    fresh[me] = total.astype(bf16)
    start, wait = along(0, lambda p: fresh.at[me], lambda p: fresh.at[p], e_send, e_recv)
    start()
    for far in range(3, parts):
        advance(far)
    finish()
    row = lax.broadcasted_iota(jnp.int32, (texts, count), 1) + me * count
    hits = jnp.concatenate(
        [jnp.where(row == spots[p][:, :1], 1.0, 0.0).astype(bf16) for p in range(groups)], axis=0
    )
    wait()
    for p in range(parts):
        rows = fresh[:, :, p * local : (p + 1) * local].reshape(groups * texts, local)
        added = lax.dot_general(hits, rows, (((0,), (0,)), ((), ())), preferred_element_type=f32)
        states[p] = (nodes[0, p].astype(f32) + added).astype(bf16)

    for layer in range(layers):
        if layer > 0:
            advance, finish = line_copies(
                nodes.at[layer], col, parts, me, cuts, line_send.at[layer], line_recv.at[layer]
            )
            for far in range(parts):
                advance(far)
        block = states if layer == 0 else nodes.at[layer]
        projected = jnp.zeros((count, local), f32)
        for p in range(parts):
            projected += jnp.dot(
                block[p], near_w[p * local : (p + 1) * local, :], preferred_element_type=f32
            )
        here = extended.at[layer]
        here[halo : halo + count, :] = projected.astype(bf16)

        @pl.when(me == 0)
        def _():
            here[0:halo, :] = jnp.zeros((halo, local), bf16)

        @pl.when(me == groups - 1)
        def _():
            here[halo + count :, :] = jnp.zeros((halo, local), bf16)

        def edge(way, incoming):
            step = 1 if way == 0 else -1
            low, high = pl.ds(0, halo), pl.ds(halo + count, halo)
            dst = here.at[low if way == 0 else high]
            src = here.at[pl.ds(count, halo) if way == 0 else pl.ds(halo, halo)]
            to = me + step
            there = (to >= 0) & (to < groups)
            if incoming:
                there = (me - step >= 0) & (me - step < groups)
                src = dst
            return there, pltpu.make_async_remote_copy(
                src_ref=src,
                dst_ref=dst,
                send_sem=halo_send.at[layer, way],
                recv_sem=halo_recv.at[layer, way],
                device_id=(to, col),
                device_id_type=MESH,
            )

        for way in range(2):
            there, copy = edge(way, False)
            pl.when(there)(copy.start)
        if layer > 0:
            finish()
        near = jnp.zeros((count, local), f32)
        for p in range(parts):
            near += jnp.dot(
                block[p], self_w[p * local : (p + 1) * local, :], preferred_element_type=f32
            )
        for way in range(2):
            there, copy = edge(way, True)
            pl.when(there)(copy.wait_recv)
        near += jnp.dot(adjacency[...], here[...], preferred_element_type=f32)
        result = jnp.maximum(near, 0.0).astype(bf16)
        for way in range(2):
            there, copy = edge(way, False)
            pl.when(there)(copy.wait_send)
        if layer < layers - 1:
            nodes[layer + 1, col] = result
        else:
            out[...] = result


def text_and_graph(
    mean, token_mean, down, embed, place, cache, adjacency, self_w, near_w
):
    groups, parts = lax.axis_size("dp"), lax.axis_size("tensor")
    texts, hidden = mean.shape
    width, (count, local) = down.shape[1], cache.shape
    features = embed.shape[1]
    sem = pltpu.SemaphoreType.DMA
    vmem = pl.BlockSpec(memory_space=pltpu.VMEM)
    cuts = 2
    return pl.pallas_call(
        functools.partial(tail_kernel, groups, parts, LAYERS, cuts),
        out_shape=jax.ShapeDtypeStruct((count, local), bf16),
        in_specs=[vmem] * 9,
        out_specs=vmem,
        scratch_shapes=[
            pltpu.VMEM((groups, texts, hidden), bf16),
            pltpu.VMEM((groups,) + place.shape, jnp.int32),
            pltpu.VMEM((groups, texts, width), f32),
            pltpu.VMEM((groups, texts, width), f32),
            pltpu.VMEM((parts, groups // parts, texts, width), f32),
            pltpu.VMEM((parts, texts, features), bf16),
            pltpu.VMEM((groups, texts, features), bf16),
            pltpu.VMEM((parts, count, local), bf16),
            pltpu.VMEM((LAYERS, parts, count, local), bf16),
            pltpu.VMEM((LAYERS, adjacency.shape[1], local), bf16),
        ]
        + [sem((groups,))] * 6
        + [sem((parts,))] * 4
        + [sem((groups,))] * 2
        + [sem((LAYERS, 2, parts - 1, cuts))] * 2
        + [sem((LAYERS, 2))] * 2,
        compiler_params=pltpu.CompilerParams(
            collective_id=1, has_side_effects=True, vmem_limit_bytes=40 << 20
        ),
        name="embed_and_layers",
    )(mean, token_mean, down, embed, place, cache, adjacency, self_w, near_w)


def per_device(
    token_states,
    norm_gain,
    gate_weight,
    up_weight,
    down_weight,
    embed_weight,
    text_owner,
    text_row,
    node_cache,
    tile_index,
    tile_live,
    tile_weight,
    self_weight,
    neighbour_weight,
):
    text_count = text_row.shape[0]
    length = token_states.shape[0] // text_count
    node_count = node_cache.shape[0]
    row_tiles, slots = tile_index.shape
    columns = row_tiles + 2 * BT
    live = (tile_index[:, :, None] == jnp.arange(columns)[None, None, :]) & (
        tile_live[:, :, None] != 0
    )
    adjacency = jnp.zeros((row_tiles, TILE, columns, TILE), f32)
    for slot in range(slots):
        adjacency += jnp.where(
            live[:, slot, None, :, None], tile_weight[:, slot, :, None, :].astype(f32), 0.0
        )
    adjacency = adjacency.astype(bf16).reshape(row_tiles * TILE, columns * TILE)
    place = jnp.broadcast_to(text_owner * node_count + text_row[:, None], (text_count, 128))
    mean, token_mean = pooled_hidden(token_states, norm_gain, gate_weight, up_weight, length)
    return text_and_graph(
        mean,
        token_mean,
        down_weight,
        embed_weight,
        place,
        node_cache,
        adjacency,
        self_weight,
        neighbour_weight,
    )


def solution(mesh):
    in_specs = (
        P("dp", "tensor"),
        P(),
        P("dp", "tensor"),
        P("dp", "tensor"),
        P("tensor", "dp"),
        P("tensor", None),
        P("dp", None),
        P("dp"),
        P("dp", "tensor"),
        P("dp", None),
        P("dp", None),
        P("dp", None, None, None),
        P(None, "tensor"),
        P(None, "tensor"),
    )
    out_specs = P("dp", "tensor")
    return jax.shard_map(
        per_device, mesh=mesh, in_specs=in_specs, out_specs=out_specs, check_vma=False
    )
```

```python
import functools

import jax
import jax.numpy as jnp
from jax import lax
from jax.experimental import pallas as pl
from jax.experimental.pallas import tpu as pltpu
from jax.sharding import PartitionSpec as P

BT = 2
LAYERS = 2

eps = 1e-05
f32 = jnp.float32
bf16 = jnp.bfloat16
MESH = pl.DeviceIdType.MESH


def flip(index, bit):
    return index + bit * (1 - 2 * ((index // bit) % 2))


def owner_of(index, mask):
    bit = 1
    while bit <= mask:
        if mask & bit:
            index = flip(index, bit)
        bit *= 2
    return index


def hop_plan(blocks, hops):
    sent, order, turn = {}, [], 0
    while len(sent) < blocks * hops:
        pick = None
        for block in range(blocks):
            for hop in range(hops):
                if (block, hop) in sent or pick is not None:
                    continue
                if hop == 0 or sent.get((block, hop - 1), turn) <= turn - 2:
                    pick = (block, hop)
        if pick is not None:
            sent[pick] = turn
        order.append(pick)
        turn += 1
    return order


def cube_plan(bits, chunks):
    came = {(array, 0, chunk): -2 for array in range(2) for chunk in range(chunks)}
    wanted = {bit: [] for bit in bits}
    for array in range(2):
        span = [0]
        for bit in bits if array == 0 else bits[::-1]:
            for chunk in range(chunks):
                wanted[bit] += [(chunk, len(span), array, mask) for mask in span]
            span = span + [mask ^ bit for mask in span]
    plan = {bit: [] for bit in bits}
    turn = 0
    while any(wanted.values()):
        arrived = []
        for bit in bits:
            ready = [
                item
                for item in sorted(wanted[bit])
                if came.get((item[2], item[3], item[0]), turn) <= turn - 2
            ]
            if ready:
                chunk, _, array, mask = ready[0]
                wanted[bit].remove(ready[0])
                plan[bit].append((array, mask, chunk))
                arrived.append((array, mask ^ bit, chunk))
            else:
                plan[bit].append(None)
        for item in arrived:
            came[item] = turn
        turn += 1
    return plan


def front_kernel(
    groups, parts, chunks, blocks, merge, length, bits, hops, cube,
    tok, gain, gw, uw, out, own_mean, whole, normed, gfull, ufull,
    hop_send, hop_recv, cube_send, cube_recv, pair_send, pair_recv, own_sem,
):
    me, col = lax.axis_index("dp"), lax.axis_index("tensor")
    depth, width = gw.shape[0], gfull.shape[2]
    rows, local = tok.shape[0] // blocks, tok.shape[1]
    feed, full = (gw, uw), (gfull, ufull)

    barrier = pltpu.get_barrier_semaphore()
    partners = [flip(me, bit) for bit in [1] + bits]
    for partner in partners:
        pl.semaphore_signal(barrier, inc=1, device_id=(partner, col), device_id_type=MESH)

    @pl.when(col > 0)
    def _():
        pl.semaphore_signal(barrier, inc=1, device_id=(me, col - 1), device_id_type=MESH)

    @pl.when(col < parts - 1)
    def _():
        pl.semaphore_signal(barrier, inc=1, device_id=(me, col + 1), device_id_type=MESH)

    own = [pltpu.make_async_copy(tok, whole.at[col], own_sem.at[0])]
    for array in range(2):
        for chunk in range(chunks):
            own.append(
                pltpu.make_async_copy(
                    feed[array].at[:, pl.ds(chunk * width, width)],
                    full[array].at[chunk, pl.ds(pl.multiple_of(me * depth, depth), depth)],
                    own_sem.at[1 + array * chunks + chunk],
                )
            )
    for copy in own:
        copy.start()

    sides = (col + parts - 1) // parts + (2 * parts - 2 - col) // parts
    pl.semaphore_wait(barrier, len(partners) + sides)

    def shard(array, mask, chunk):
        at = pl.multiple_of(owner_of(me, mask) * depth, depth)
        return full[array].at[chunk, pl.ds(at, depth)]

    def swap(array, mask, chunk, bit, send, recv):
        src = shard(array, mask, chunk)
        if mask == 0:
            src = feed[array].at[:, pl.ds(chunk * width, width)]
        return pltpu.make_async_remote_copy(
            src_ref=src,
            dst_ref=shard(array, mask, chunk),
            send_sem=send,
            recv_sem=recv,
            device_id=(flip(me, bit), col),
            device_id_type=MESH,
        )

    def landed(array, mask, chunk, bit, send, recv):
        there = shard(array, mask ^ bit, chunk)
        return pltpu.make_async_remote_copy(
            src_ref=there,
            dst_ref=there,
            send_sem=send,
            recv_sem=recv,
            device_id=(flip(me, bit), col),
            device_id_type=MESH,
        )

    def hop(turn, way, incoming):
        block, far = hops[turn]
        step = 1 if way == 0 else -1
        held = col - step * far
        if incoming:
            held = col - step * (far + 1)
            there = (held >= 0) & (held < parts)
        else:
            there = (held >= 0) & (held < parts) & (col + step >= 0) & (col + step < parts)
        span = pl.ds(block * rows, rows)
        src = whole.at[held, span]
        if not incoming and far == 0:
            src = tok.at[span]
        copy = pltpu.make_async_remote_copy(
            src_ref=src,
            dst_ref=whole.at[held, span],
            send_sem=hop_send.at[way, turn],
            recv_sem=hop_recv.at[way, turn],
            device_id=(me, col + step),
            device_id_type=MESH,
        )
        return there, copy

    def pair(array, mask, chunk):
        at = (array * (groups // 2) + mask // 2) * chunks + chunk
        return array, mask, chunk, 1, pair_send.at[at], pair_recv.at[at]

    def normalise(block):
        def one(part, _):
            span = pl.ds(pl.multiple_of(block * rows + part * length, length), length)
            square = jnp.zeros((length, 1), f32)
            for p in range(parts):
                wide = whole[p, span, :].astype(f32)
                square += jnp.sum(wide * wide, axis=1, keepdims=True)
            scale = lax.rsqrt(square * (1.0 / (parts * local)) + eps)
            for p in range(parts):
                wide = whole[p, span, :].astype(f32)
                normed[span, p * local : (p + 1) * local] = (
                    wide * scale * gain[:, p * local : (p + 1) * local].astype(f32)
                ).astype(bf16)
            return 0

        lax.fori_loop(0, rows // length, one, 0)

    def work(block, chunk):
        tall = rows * merge
        x = normed[pl.ds(pl.multiple_of(block * tall, tall), tall), :]
        gate = jnp.dot(x, gfull[chunk], preferred_element_type=f32)
        upward = jnp.dot(x, ufull[chunk], preferred_element_type=f32)
        hidden = (gate / (1.0 + jnp.exp(-gate)) * upward).astype(bf16).astype(f32)
        mean = jnp.sum(hidden.reshape(tall // length, length, width), axis=1)
        out[chunk, block] = mean * (1.0 / length)

    turns = max([len(hops)] + [len(cube[bit]) for bit in bits])
    missing = {chunk: 2 * groups for chunk in range(chunks)}
    unhopped = {block: parts - 1 for block in range(blocks)}
    ready_chunks, ready_blocks, came = [], [], []
    flying = []

    for array in range(2):
        for chunk in range(chunks):
            swap(*pair(array, 0, chunk)).start()
            flying.append((array, 0, chunk))
    for turn in range(turns + 3):
        back = turn - 2
        new_blocks, new_chunks = [], []
        settled = flying
        flying = []
        if 0 <= back < turns:
            if back < len(hops) and hops[back] is not None:
                for way in range(2):
                    there, copy = hop(back, way, True)
                    pl.when(there)(copy.wait_recv)
                    there, copy = hop(back, way, False)
                    pl.when(there)(copy.wait_send)
                unhopped[hops[back][0]] -= 1
                if unhopped[hops[back][0]] == 0:
                    new_blocks.append(hops[back][0])
            for n, bit in enumerate(bits):
                item = cube[bit][back] if back < len(cube[bit]) else None
                if item is not None:
                    sems = (cube_send.at[n, back], cube_recv.at[n, back])
                    landed(*item, bit, *sems).wait_recv()
                    swap(*item, bit, *sems).wait_send()
                    moved = (item[0], item[1] ^ bit, item[2])
                    swap(*pair(*moved)).start()
                    flying.append(moved)
        if turn < len(hops) and hops[turn] is not None:
            for way in range(2):
                there, copy = hop(turn, way, False)
                pl.when(there)(copy.start)
        for n, bit in enumerate(bits):
            item = cube[bit][turn] if turn < len(cube[bit]) else None
            if item is not None:
                swap(*item, bit, cube_send.at[n, turn], cube_recv.at[n, turn]).start()
        if turn == 0:
            for copy in own:
                copy.wait()

            def average(text, _):
                span = pl.ds(pl.multiple_of(text * length, length), length)
                own_mean[text] = jnp.sum(
                    whole[col, span, :].astype(f32), axis=0, keepdims=True
                ) * (1.0 / length)
                return 0

            lax.fori_loop(0, tok.shape[0] // length, average, 0)
            for chunk in range(chunks):
                missing[chunk] -= 2
        for block in new_blocks:
            normalise(block)
            came.append(block)
            block = block // merge
            if not all(block * merge + n in came for n in range(merge)):
                continue
            if ready_chunks:
                def across(n, _, block=block):
                    work(block, n)
                    return 0
                lax.fori_loop(0, len(ready_chunks), across, 0)
            ready_blocks.append(block)
        for array, mask, chunk in settled:
            landed(*pair(array, mask, chunk)).wait_recv()
            swap(*pair(array, mask, chunk)).wait_send()
            missing[chunk] -= 1
        for array, mask, chunk in settled:
            if mask:
                missing[chunk] -= 1
        for chunk in range(chunks):
            if missing[chunk] == 0 and chunk not in ready_chunks:
                assert chunk == len(ready_chunks)
                if ready_blocks:
                    assert ready_blocks == list(range(len(ready_blocks)))
                    def down(n, _, chunk=chunk):
                        work(n, chunk)
                        return 0
                    lax.fori_loop(0, len(ready_blocks), down, 0)
                ready_chunks.append(chunk)
    assert len(ready_chunks) == chunks and len(ready_blocks) == blocks // merge and not flying


def pooled_hidden(token_states, norm_gain, gate_weight, up_weight, length):
    groups, parts = lax.axis_size("dp"), lax.axis_size("tensor")
    tokens, local = token_states.shape
    depth, hidden = gate_weight.shape
    chunks = blocks = 8
    merge = 2
    width, rows = hidden // chunks, tokens // blocks
    bits = [1 << n for n in range(1, (groups - 1).bit_length())]
    hops = hop_plan(blocks, parts - 1)
    cube = cube_plan(bits, chunks)
    turns = max(len(cube[bit]) for bit in bits)
    pairs = 2 * chunks * (groups // 2)
    sem = pltpu.SemaphoreType.DMA
    features = parts * local
    any_space = pl.BlockSpec(memory_space=pl.ANY)
    vmem = pl.BlockSpec(memory_space=pltpu.VMEM)
    mean, own_mean = pl.pallas_call(
        functools.partial(
            front_kernel, groups, parts, chunks, blocks, merge, length, bits, hops, cube
        ),
        out_shape=[
            jax.ShapeDtypeStruct((chunks, blocks // merge, rows * merge // length, width), f32),
            jax.ShapeDtypeStruct((tokens // length, 1, local), f32),
        ],
        in_specs=[any_space, vmem, any_space, any_space],
        out_specs=[vmem, vmem],
        scratch_shapes=[
            pltpu.VMEM((parts, tokens, local), bf16),
            pltpu.VMEM((tokens, features), bf16),
            pltpu.VMEM((chunks, groups * depth, width), bf16),
            pltpu.VMEM((chunks, groups * depth, width), bf16),
            sem((2, len(hops))),
            sem((2, len(hops))),
            sem((len(bits), turns)),
            sem((len(bits), turns)),
            sem((pairs,)),
            sem((pairs,)),
            sem((1 + 2 * chunks,)),
        ],
        compiler_params=pltpu.CompilerParams(
            collective_id=0, has_side_effects=True, vmem_limit_bytes=48 << 20
        ),
        cost_estimate=pl.CostEstimate(
            flops=4 * tokens * features * hidden,
            bytes_accessed=4 * features * hidden,
            transcendentals=tokens * hidden,
        ),
        name="gather_and_pool",
    )(token_states, norm_gain[None], gate_weight, up_weight)
    mean = jnp.transpose(mean, (1, 2, 0, 3)).reshape(tokens // length, hidden)
    return mean, own_mean[:, 0]


def line_copies(buffer, col, parts, me, cuts, send, recv):
    size = buffer.shape[1] // cuts

    def copy(way, far, cut, incoming):
        step = 1 if way == 0 else -1
        held = col - step * (far + 1 if incoming else far)
        there = (held >= 0) & (held < parts)
        if not incoming:
            there = there & (col + step >= 0) & (col + step < parts)
        part = buffer.at[held, pl.ds(cut * size, size)]
        return there, pltpu.make_async_remote_copy(
            src_ref=part,
            dst_ref=part,
            send_sem=send.at[way, far, cut],
            recv_sem=recv.at[way, far, cut],
            device_id=(me, col + step),
            device_id_type=MESH,
        )

    def advance(far):
        for cut in range(cuts):
            for way in range(2):
                if far > 0:
                    there, came = copy(way, far - 1, cut, True)
                    pl.when(there)(came.wait_recv)
                if far < parts - 1:
                    there, gone = copy(way, far, cut, False)
                    pl.when(there)(gone.start)

    def finish():
        for far in range(parts - 1):
            for cut in range(cuts):
                for way in range(2):
                    there, gone = copy(way, far, cut, False)
                    pl.when(there)(gone.wait_send)

    return advance, finish


def tail_kernel(
    groups, parts, layers, cuts,
    mean, token_mean, down, embed, place, cache, index, live, tiles, self_w, near_w, out,
    adjacency, hidden, spots, share, pooled, terms, sums, fresh, states, nodes, extended,
    a_send, a_recv, p_send, p_recv, b_send, b_recv, c_send, c_recv,
    d_send, d_recv, e_send, e_recv, line_send, line_recv, halo_send, halo_recv,
):
    me, col = lax.axis_index("dp"), lax.axis_index("tensor")
    texts, width = mean.shape[0], down.shape[1]
    count, local = cache.shape
    halo = (extended.shape[1] - count) // 2
    split = groups // parts

    barrier = pltpu.get_barrier_semaphore()
    for s in range(1, groups):
        pl.semaphore_signal(
            barrier, inc=1, device_id=((me + s) % groups, col), device_id_type=MESH
        )
    for s in range(1, parts):
        pl.semaphore_signal(
            barrier, inc=1, device_id=(me, (col + s) % parts), device_id_type=MESH
        )
    hidden[me] = mean[...].astype(bf16)
    spots[me] = place[...]
    nodes[0, col] = cache[...]
    pl.semaphore_wait(barrier, groups + parts - 2)

    def along(axis, src, dst, send, recv):
        size = groups if axis == 0 else parts
        mine = me if axis == 0 else col

        def copy(s, incoming):
            peer = (mine + s) % size
            slot = dst(mine)
            if incoming:
                slot = dst((mine + size - s) % size)
            return pltpu.make_async_remote_copy(
                src_ref=slot if incoming else src(peer),
                dst_ref=slot,
                send_sem=send.at[s],
                recv_sem=recv.at[s],
                device_id=(peer, col) if axis == 0 else (me, peer),
                device_id_type=MESH,
            )

        def start():
            for s in range(1, size):
                copy(s, False).start()

        def wait():
            for s in range(1, size):
                copy(s, True).wait_recv()
            for s in range(1, size):
                copy(s, False).wait_send()

        return start, wait

    advance, finish = line_copies(
        nodes.at[0], col, parts, me, cuts, line_send.at[0], line_recv.at[0]
    )
    start_a, wait_a = along(0, lambda p: hidden.at[me], lambda p: hidden.at[p], a_send, a_recv)
    start_p, wait_p = along(0, lambda p: spots.at[me], lambda p: spots.at[p], p_send, p_recv)
    start_a()
    start_p()
    advance(0)
    row_tiles, slots, tile = tiles.shape[0], tiles.shape[1], tiles.shape[2]

    def fill(r, _):
        rows = pl.ds(pl.multiple_of(r * tile, tile), tile)
        for c in range(adjacency.shape[1] // tile):
            total = jnp.zeros((tile, tile), f32)
            for k in range(slots):
                weight = jnp.where(index[r, k] == c, live[r, k], 0).astype(f32)
                total += weight * tiles[r, k].astype(f32)
            adjacency[rows, c * tile : (c + 1) * tile] = total.astype(bf16)
        return 0

    lax.fori_loop(0, row_tiles, fill, 0)
    wait_a()
    wait_p()
    advance(1)
    part = jnp.dot(
        hidden[...].reshape(groups * texts, hidden.shape[2]),
        down[...],
        preferred_element_type=f32,
    )
    share[...] = part.reshape(groups, texts, width)
    pooled[me] = share[me]
    start, wait = along(0, lambda p: share.at[p], lambda p: pooled.at[p], b_send, b_recv)
    start()
    wait()
    terms[col] = pooled[pl.ds(col * split, split)]
    start, wait = along(
        1, lambda p: pooled.at[pl.ds(p * split, split)], lambda p: terms.at[p], c_send, c_recv
    )
    start()
    if parts > 2:
        advance(2)
    wait()
    total = jnp.zeros((texts, embed.shape[1]), f32)
    for i in range(split):
        value = token_mean[:, i * width : (i + 1) * width]
        for p in range(parts):
            value += terms[p, i]
        high = value.astype(bf16)
        low = (value - high.astype(f32)).astype(bf16)
        rows = embed[i * width : (i + 1) * width, :]
        total += jnp.dot(high, rows, preferred_element_type=f32)
        total += jnp.dot(low, rows, preferred_element_type=f32)
    sums[col] = total.astype(bf16)
    start, wait = along(1, lambda p: sums.at[col], lambda p: sums.at[p], d_send, d_recv)
    start()
    wait()
    total = jnp.zeros((texts, embed.shape[1]), f32)
    for p in range(parts):
        total += sums[p].astype(f32)
    fresh[me] = total.astype(bf16)
    start, wait = along(0, lambda p: fresh.at[me], lambda p: fresh.at[p], e_send, e_recv)
    start()
    for far in range(3, parts):
        advance(far)
    finish()
    row = lax.broadcasted_iota(jnp.int32, (texts, count), 1) + me * count
    hits = jnp.concatenate(
        [jnp.where(row == spots[p][:, :1], 1.0, 0.0).astype(bf16) for p in range(groups)], axis=0
    )
    wait()
    for p in range(parts):
        rows = fresh[:, :, p * local : (p + 1) * local].reshape(groups * texts, local)
        added = lax.dot_general(hits, rows, (((0,), (0,)), ((), ())), preferred_element_type=f32)
        states[p] = (nodes[0, p].astype(f32) + added).astype(bf16)

    for layer in range(layers):
        if layer > 0:
            advance, finish = line_copies(
                nodes.at[layer], col, parts, me, cuts, line_send.at[layer], line_recv.at[layer]
            )
            for far in range(parts):
                advance(far)
        block = states if layer == 0 else nodes.at[layer]
        projected = jnp.zeros((count, local), f32)
        for p in range(parts):
            projected += jnp.dot(
                block[p], near_w[p * local : (p + 1) * local, :], preferred_element_type=f32
            )
        here = extended.at[layer]
        here[halo : halo + count, :] = projected.astype(bf16)

        @pl.when(me == 0)
        def _():
            here[0:halo, :] = jnp.zeros((halo, local), bf16)

        @pl.when(me == groups - 1)
        def _():
            here[halo + count :, :] = jnp.zeros((halo, local), bf16)

        def edge(way, incoming):
            step = 1 if way == 0 else -1
            low, high = pl.ds(0, halo), pl.ds(halo + count, halo)
            dst = here.at[low if way == 0 else high]
            src = here.at[pl.ds(count, halo) if way == 0 else pl.ds(halo, halo)]
            to = me + step
            there = (to >= 0) & (to < groups)
            if incoming:
                there = (me - step >= 0) & (me - step < groups)
                src = dst
            return there, pltpu.make_async_remote_copy(
                src_ref=src,
                dst_ref=dst,
                send_sem=halo_send.at[layer, way],
                recv_sem=halo_recv.at[layer, way],
                device_id=(to, col),
                device_id_type=MESH,
            )

        for way in range(2):
            there, copy = edge(way, False)
            pl.when(there)(copy.start)
        if layer > 0:
            finish()
        near = jnp.zeros((count, local), f32)
        for p in range(parts):
            near += jnp.dot(
                block[p], self_w[p * local : (p + 1) * local, :], preferred_element_type=f32
            )
        for way in range(2):
            there, copy = edge(way, True)
            pl.when(there)(copy.wait_recv)
        near += jnp.dot(adjacency[...], here[...], preferred_element_type=f32)
        result = jnp.maximum(near, 0.0).astype(bf16)
        for way in range(2):
            there, copy = edge(way, False)
            pl.when(there)(copy.wait_send)
        if layer < layers - 1:
            nodes[layer + 1, col] = result
        else:
            out[...] = result


def text_and_graph(
    mean, token_mean, down, embed, place, cache, index, live, tiles, self_w, near_w
):
    groups, parts = lax.axis_size("dp"), lax.axis_size("tensor")
    texts, hidden = mean.shape
    width, (count, local) = down.shape[1], cache.shape
    features = embed.shape[1]
    sem = pltpu.SemaphoreType.DMA
    vmem = pl.BlockSpec(memory_space=pltpu.VMEM)
    cuts = 2
    smem = pl.BlockSpec(memory_space=pltpu.SMEM)
    reach = count + 2 * BT * tiles.shape[2]
    return pl.pallas_call(
        functools.partial(tail_kernel, groups, parts, LAYERS, cuts),
        out_shape=jax.ShapeDtypeStruct((count, local), bf16),
        in_specs=[vmem] * 6 + [smem] * 2 + [vmem] * 3,
        out_specs=vmem,
        scratch_shapes=[
            pltpu.VMEM((count, reach), bf16),
            pltpu.VMEM((groups, texts, hidden), bf16),
            pltpu.VMEM((groups,) + place.shape, jnp.int32),
            pltpu.VMEM((groups, texts, width), f32),
            pltpu.VMEM((groups, texts, width), f32),
            pltpu.VMEM((parts, groups // parts, texts, width), f32),
            pltpu.VMEM((parts, texts, features), bf16),
            pltpu.VMEM((groups, texts, features), bf16),
            pltpu.VMEM((parts, count, local), bf16),
            pltpu.VMEM((LAYERS, parts, count, local), bf16),
            pltpu.VMEM((LAYERS, reach, local), bf16),
        ]
        + [sem((groups,))] * 6
        + [sem((parts,))] * 4
        + [sem((groups,))] * 2
        + [sem((LAYERS, 2, parts - 1, cuts))] * 2
        + [sem((LAYERS, 2))] * 2,
        compiler_params=pltpu.CompilerParams(
            collective_id=1, has_side_effects=True, vmem_limit_bytes=40 << 20
        ),
        name="embed_and_layers",
    )(mean, token_mean, down, embed, place, cache, index, live, tiles, self_w, near_w)


def per_device(
    token_states,
    norm_gain,
    gate_weight,
    up_weight,
    down_weight,
    embed_weight,
    text_owner,
    text_row,
    node_cache,
    tile_index,
    tile_live,
    tile_weight,
    self_weight,
    neighbour_weight,
):
    text_count = text_row.shape[0]
    length = token_states.shape[0] // text_count
    node_count = node_cache.shape[0]
    place = jnp.broadcast_to(text_owner * node_count + text_row[:, None], (text_count, 128))
    mean, token_mean = pooled_hidden(token_states, norm_gain, gate_weight, up_weight, length)
    return text_and_graph(
        mean,
        token_mean,
        down_weight,
        embed_weight,
        place,
        node_cache,
        tile_index,
        tile_live,
        tile_weight,
        self_weight,
        neighbour_weight,
    )


def solution(mesh):
    in_specs = (
        P("dp", "tensor"),
        P(),
        P("dp", "tensor"),
        P("dp", "tensor"),
        P("tensor", "dp"),
        P("tensor", None),
        P("dp", None),
        P("dp"),
        P("dp", "tensor"),
        P("dp", None),
        P("dp", None),
        P("dp", None, None, None),
        P(None, "tensor"),
        P(None, "tensor"),
    )
    out_specs = P("dp", "tensor")
    return jax.shard_map(
        per_device, mesh=mesh, in_specs=in_specs, out_specs=out_specs, check_vma=False
    )
```

```python
import functools

import jax
import jax.numpy as jnp
from jax import lax
from jax.experimental import pallas as pl
from jax.experimental.pallas import tpu as pltpu
from jax.sharding import PartitionSpec as P

BT = 2
LAYERS = 2

eps = 1e-05
f32 = jnp.float32
bf16 = jnp.bfloat16
MESH = pl.DeviceIdType.MESH


def flip(index, bit):
    return index + bit * (1 - 2 * ((index // bit) % 2))


def owner_of(index, mask):
    bit = 1
    while bit <= mask:
        if mask & bit:
            index = flip(index, bit)
        bit *= 2
    return index


def hop_plan(blocks, hops):
    sent, order, turn = {}, [], 0
    while len(sent) < blocks * hops:
        pick = None
        for block in range(blocks):
            for hop in range(hops):
                if (block, hop) in sent or pick is not None:
                    continue
                if hop == 0 or sent.get((block, hop - 1), turn) <= turn - 2:
                    pick = (block, hop)
        if pick is not None:
            sent[pick] = turn
        order.append(pick)
        turn += 1
    return order


def cube_plan(bits, chunks):
    came = {(array, 0, chunk): -2 for array in range(2) for chunk in range(chunks)}
    wanted = {bit: [] for bit in bits}
    for array in range(2):
        span = [0]
        for bit in bits if array == 0 else bits[::-1]:
            for chunk in range(chunks):
                wanted[bit] += [(chunk, len(span), array, mask) for mask in span]
            span = span + [mask ^ bit for mask in span]
    plan = {bit: [] for bit in bits}
    turn = 0
    while any(wanted.values()):
        arrived = []
        for bit in bits:
            ready = [
                item
                for item in sorted(wanted[bit])
                if came.get((item[2], item[3], item[0]), turn) <= turn - 2
            ]
            if ready:
                chunk, _, array, mask = ready[0]
                wanted[bit].remove(ready[0])
                plan[bit].append((array, mask, chunk))
                arrived.append((array, mask ^ bit, chunk))
            else:
                plan[bit].append(None)
        for item in arrived:
            came[item] = turn
        turn += 1
    return plan


def front_kernel(
    groups, parts, chunks, blocks, merge, length, bits, hops, cube,
    tok, gain, gw, uw, index, live, stored, out, own_mean, adjacency, whole, normed, gfull, ufull,
    hop_send, hop_recv, cube_send, cube_recv, pair_send, pair_recv, own_sem, tiles,
):
    me, col = lax.axis_index("dp"), lax.axis_index("tensor")
    depth, width = gw.shape[0], gfull.shape[2]
    rows, local = tok.shape[0] // blocks, tok.shape[1]
    feed, full = (gw, uw), (gfull, ufull)

    barrier = pltpu.get_barrier_semaphore()
    partners = [flip(me, bit) for bit in [1] + bits]
    for partner in partners:
        pl.semaphore_signal(barrier, inc=1, device_id=(partner, col), device_id_type=MESH)

    @pl.when(col > 0)
    def _():
        pl.semaphore_signal(barrier, inc=1, device_id=(me, col - 1), device_id_type=MESH)

    @pl.when(col < parts - 1)
    def _():
        pl.semaphore_signal(barrier, inc=1, device_id=(me, col + 1), device_id_type=MESH)

    own = [pltpu.make_async_copy(tok, whole.at[col], own_sem.at[0])]
    for array in range(2):
        for chunk in range(chunks):
            own.append(
                pltpu.make_async_copy(
                    feed[array].at[:, pl.ds(chunk * width, width)],
                    full[array].at[chunk, pl.ds(pl.multiple_of(me * depth, depth), depth)],
                    own_sem.at[1 + array * chunks + chunk],
                )
            )
    own.append(pltpu.make_async_copy(stored, tiles, own_sem.at[1 + 2 * chunks]))
    for copy in own:
        copy.start()

    sides = (col + parts - 1) // parts + (2 * parts - 2 - col) // parts
    pl.semaphore_wait(barrier, len(partners) + sides)

    def shard(array, mask, chunk):
        at = pl.multiple_of(owner_of(me, mask) * depth, depth)
        return full[array].at[chunk, pl.ds(at, depth)]

    def swap(array, mask, chunk, bit, send, recv):
        src = shard(array, mask, chunk)
        if mask == 0:
            src = feed[array].at[:, pl.ds(chunk * width, width)]
        return pltpu.make_async_remote_copy(
            src_ref=src,
            dst_ref=shard(array, mask, chunk),
            send_sem=send,
            recv_sem=recv,
            device_id=(flip(me, bit), col),
            device_id_type=MESH,
        )

    def landed(array, mask, chunk, bit, send, recv):
        there = shard(array, mask ^ bit, chunk)
        return pltpu.make_async_remote_copy(
            src_ref=there,
            dst_ref=there,
            send_sem=send,
            recv_sem=recv,
            device_id=(flip(me, bit), col),
            device_id_type=MESH,
        )

    def hop(turn, way, incoming):
        block, far = hops[turn]
        step = 1 if way == 0 else -1
        held = col - step * far
        if incoming:
            held = col - step * (far + 1)
            there = (held >= 0) & (held < parts)
        else:
            there = (held >= 0) & (held < parts) & (col + step >= 0) & (col + step < parts)
        span = pl.ds(block * rows, rows)
        src = whole.at[held, span]
        if not incoming and far == 0:
            src = tok.at[span]
        copy = pltpu.make_async_remote_copy(
            src_ref=src,
            dst_ref=whole.at[held, span],
            send_sem=hop_send.at[way, turn],
            recv_sem=hop_recv.at[way, turn],
            device_id=(me, col + step),
            device_id_type=MESH,
        )
        return there, copy

    def pair(array, mask, chunk):
        at = (array * (groups // 2) + mask // 2) * chunks + chunk
        return array, mask, chunk, 1, pair_send.at[at], pair_recv.at[at]

    def normalise(block):
        def one(part, _):
            span = pl.ds(pl.multiple_of(block * rows + part * length, length), length)
            square = jnp.zeros((length, 1), f32)
            for p in range(parts):
                wide = whole[p, span, :].astype(f32)
                square += jnp.sum(wide * wide, axis=1, keepdims=True)
            scale = lax.rsqrt(square * (1.0 / (parts * local)) + eps)
            for p in range(parts):
                wide = whole[p, span, :].astype(f32)
                normed[span, p * local : (p + 1) * local] = (
                    wide * scale * gain[:, p * local : (p + 1) * local].astype(f32)
                ).astype(bf16)
            return 0

        lax.fori_loop(0, rows // length, one, 0)

    def work(block, chunk, many=1):
        tall = rows * merge * many
        x = normed[pl.ds(pl.multiple_of(block * rows * merge, rows), tall), :]
        gate = jnp.dot(x, gfull[chunk], preferred_element_type=f32)
        upward = jnp.dot(x, ufull[chunk], preferred_element_type=f32)
        hidden = (gate / (1.0 + jnp.exp(-gate)) * upward).astype(bf16).astype(f32)
        mean = jnp.sum(hidden.reshape(tall // length, length, width), axis=1)
        mean = (mean * (1.0 / length)).reshape((many,) + out.shape[2:])
        out[chunk, pl.ds(block, many)] = mean

    turns = max([len(hops)] + [len(cube[bit]) for bit in bits])
    missing = {chunk: 2 * groups for chunk in range(chunks)}
    unhopped = {block: parts - 1 for block in range(blocks)}
    ready_chunks, ready_blocks, came = [], [], []
    flying = []

    for array in range(2):
        for chunk in range(chunks):
            swap(*pair(array, 0, chunk)).start()
            flying.append((array, 0, chunk))
    for turn in range(turns + 3):
        back = turn - 2
        new_blocks, new_chunks = [], []
        settled = flying
        flying = []
        if 0 <= back < turns:
            if back < len(hops) and hops[back] is not None:
                for way in range(2):
                    there, copy = hop(back, way, True)
                    pl.when(there)(copy.wait_recv)
                    there, copy = hop(back, way, False)
                    pl.when(there)(copy.wait_send)
                unhopped[hops[back][0]] -= 1
                if unhopped[hops[back][0]] == 0:
                    new_blocks.append(hops[back][0])
            for n, bit in enumerate(bits):
                item = cube[bit][back] if back < len(cube[bit]) else None
                if item is not None:
                    sems = (cube_send.at[n, back], cube_recv.at[n, back])
                    landed(*item, bit, *sems).wait_recv()
                    swap(*item, bit, *sems).wait_send()
                    moved = (item[0], item[1] ^ bit, item[2])
                    swap(*pair(*moved)).start()
                    flying.append(moved)
        if turn < len(hops) and hops[turn] is not None:
            for way in range(2):
                there, copy = hop(turn, way, False)
                pl.when(there)(copy.start)
        for n, bit in enumerate(bits):
            item = cube[bit][turn] if turn < len(cube[bit]) else None
            if item is not None:
                swap(*item, bit, cube_send.at[n, turn], cube_recv.at[n, turn]).start()
        if turn == 0:
            for copy in own:
                copy.wait()

            def average(text, _):
                span = pl.ds(pl.multiple_of(text * length, length), length)
                own_mean[text] = jnp.sum(
                    whole[col, span, :].astype(f32), axis=0, keepdims=True
                ) * (1.0 / length)
                return 0

            lax.fori_loop(0, tok.shape[0] // length, average, 0)
            row_tiles, slots, tile = tiles.shape[0], tiles.shape[1], tiles.shape[2]

            def fill(r, _):
                rows = pl.ds(pl.multiple_of(r * tile, tile), tile)
                for c in range(adjacency.shape[1] // tile):
                    total = jnp.zeros((tile, tile), f32)
                    for k in range(slots):
                        weight = jnp.where(index[r, k] == c, live[r, k], 0).astype(f32)
                        total += weight * tiles[r, k].astype(f32)
                    adjacency[rows, c * tile : (c + 1) * tile] = total.astype(bf16)
                return 0

            lax.fori_loop(0, row_tiles, fill, 0)
            for chunk in range(chunks):
                missing[chunk] -= 2
        for block in new_blocks:
            normalise(block)
            came.append(block)
            block = block // merge
            if not all(block * merge + n in came for n in range(merge)):
                continue
            if ready_chunks:
                def across(n, _, block=block):
                    work(block, n)
                    return 0
                lax.fori_loop(0, len(ready_chunks), across, 0)
            ready_blocks.append(block)
        for array, mask, chunk in settled:
            landed(*pair(array, mask, chunk)).wait_recv()
            swap(*pair(array, mask, chunk)).wait_send()
            missing[chunk] -= 1
        for array, mask, chunk in settled:
            if mask:
                missing[chunk] -= 1
        for chunk in range(chunks):
            if missing[chunk] == 0 and chunk not in ready_chunks:
                assert chunk == len(ready_chunks)
                if ready_blocks:
                    assert ready_blocks == list(range(len(ready_blocks)))
                    def down(n, _, chunk=chunk):
                        work(2 * n, chunk, 2)
                        return 0
                    lax.fori_loop(0, len(ready_blocks) // 2, down, 0)
                    if len(ready_blocks) % 2:
                        work(len(ready_blocks) - 1, chunk)
                ready_chunks.append(chunk)
    assert len(ready_chunks) == chunks and len(ready_blocks) == blocks // merge and not flying


def pooled_hidden(
    token_states, norm_gain, gate_weight, up_weight, index, live, tile_weight, length
):
    groups, parts = lax.axis_size("dp"), lax.axis_size("tensor")
    tokens, local = token_states.shape
    depth, hidden = gate_weight.shape
    chunks = blocks = 4
    merge = 1
    width, rows = hidden // chunks, tokens // blocks
    bits = [1 << n for n in range(1, (groups - 1).bit_length())]
    hops = hop_plan(blocks, parts - 1)
    cube = cube_plan(bits, chunks)
    turns = max(len(cube[bit]) for bit in bits)
    pairs = 2 * chunks * (groups // 2)
    sem = pltpu.SemaphoreType.DMA
    features = parts * local
    hbm = pl.BlockSpec(memory_space=pltpu.HBM)
    smem = pl.BlockSpec(memory_space=pltpu.SMEM)
    row_tiles, _, tile, _ = tile_weight.shape
    nodes = row_tiles * tile
    vmem = pl.BlockSpec(memory_space=pltpu.VMEM)
    mean, own_mean, adjacency = pl.pallas_call(
        functools.partial(
            front_kernel, groups, parts, chunks, blocks, merge, length, bits, hops, cube
        ),
        out_shape=[
            jax.ShapeDtypeStruct((chunks, blocks // merge, rows * merge // length, width), f32),
            jax.ShapeDtypeStruct((tokens // length, 1, local), f32),
            jax.ShapeDtypeStruct((nodes, nodes + 2 * BT * tile), bf16),
        ],
        in_specs=[hbm, vmem, hbm, hbm, smem, smem, hbm],
        out_specs=[vmem, vmem, vmem],
        scratch_shapes=[
            pltpu.VMEM((parts, tokens, local), bf16),
            pltpu.VMEM((tokens, features), bf16),
            pltpu.VMEM((chunks, groups * depth, width), bf16),
            pltpu.VMEM((chunks, groups * depth, width), bf16),
            sem((2, len(hops))),
            sem((2, len(hops))),
            sem((len(bits), turns)),
            sem((len(bits), turns)),
            sem((pairs,)),
            sem((pairs,)),
            sem((2 + 2 * chunks,)),
            pltpu.VMEM(tile_weight.shape, bf16),
        ],
        compiler_params=pltpu.CompilerParams(
            collective_id=0, has_side_effects=True, vmem_limit_bytes=56 << 20
        ),
        cost_estimate=pl.CostEstimate(
            flops=4 * tokens * features * hidden,
            bytes_accessed=4 * features * hidden,
            transcendentals=tokens * hidden,
        ),
        name="gather_and_pool",
    )(token_states, norm_gain[None], gate_weight, up_weight, index, live, tile_weight)
    mean = jnp.transpose(mean, (1, 2, 0, 3)).reshape(tokens // length, hidden)
    return mean, own_mean[:, 0], adjacency


def line_copies(buffer, col, parts, me, cuts, send, recv):
    size = buffer.shape[1] // cuts

    def copy(way, far, cut, incoming):
        step = 1 if way == 0 else -1
        held = col - step * (far + 1 if incoming else far)
        there = (held >= 0) & (held < parts)
        if not incoming:
            there = there & (col + step >= 0) & (col + step < parts)
        part = buffer.at[held, pl.ds(cut * size, size)]
        return there, pltpu.make_async_remote_copy(
            src_ref=part,
            dst_ref=part,
            send_sem=send.at[way, far, cut],
            recv_sem=recv.at[way, far, cut],
            device_id=(me, col + step),
            device_id_type=MESH,
        )

    def advance(far):
        for cut in range(cuts):
            for way in range(2):
                if far > 0:
                    there, came = copy(way, far - 1, cut, True)
                    pl.when(there)(came.wait_recv)
                if far < parts - 1:
                    there, gone = copy(way, far, cut, False)
                    pl.when(there)(gone.start)

    def finish():
        for far in range(parts - 1):
            for cut in range(cuts):
                for way in range(2):
                    there, gone = copy(way, far, cut, False)
                    pl.when(there)(gone.wait_send)

    return advance, finish


def tail_kernel(
    groups, parts, layers, cuts,
    mean, token_mean, down, embed, place, cache, adjacency, self_w, near_w, out,
    hidden, spots, share, pooled, terms, sums, fresh, states, nodes, extended,
    a_send, a_recv, p_send, p_recv, b_send, b_recv, c_send, c_recv,
    d_send, d_recv, e_send, e_recv, line_send, line_recv, halo_send, halo_recv,
):
    me, col = lax.axis_index("dp"), lax.axis_index("tensor")
    texts, width = mean.shape[0], down.shape[1]
    count, local = cache.shape
    halo = (extended.shape[1] - count) // 2
    split = groups // parts

    barrier = pltpu.get_barrier_semaphore()
    for s in range(1, groups):
        pl.semaphore_signal(
            barrier, inc=1, device_id=((me + s) % groups, col), device_id_type=MESH
        )
    for s in range(1, parts):
        pl.semaphore_signal(
            barrier, inc=1, device_id=(me, (col + s) % parts), device_id_type=MESH
        )
    hidden[me] = mean[...].astype(bf16)
    spots[me] = place[...]
    nodes[0, col] = cache[...]
    pl.semaphore_wait(barrier, groups + parts - 2)

    def along(axis, src, dst, send, recv):
        size = groups if axis == 0 else parts
        mine = me if axis == 0 else col

        def copy(s, incoming):
            peer = (mine + s) % size
            slot = dst(mine)
            if incoming:
                slot = dst((mine + size - s) % size)
            return pltpu.make_async_remote_copy(
                src_ref=slot if incoming else src(peer),
                dst_ref=slot,
                send_sem=send.at[s],
                recv_sem=recv.at[s],
                device_id=(peer, col) if axis == 0 else (me, peer),
                device_id_type=MESH,
            )

        def start():
            for s in range(1, size):
                copy(s, False).start()

        def wait():
            for s in range(1, size):
                copy(s, True).wait_recv()
            for s in range(1, size):
                copy(s, False).wait_send()

        return start, wait

    advance, finish = line_copies(
        nodes.at[0], col, parts, me, cuts, line_send.at[0], line_recv.at[0]
    )
    start_a, wait_a = along(0, lambda p: hidden.at[me], lambda p: hidden.at[p], a_send, a_recv)
    start_p, wait_p = along(0, lambda p: spots.at[me], lambda p: spots.at[p], p_send, p_recv)
    start_a()
    start_p()
    advance(0)
    wait_a()
    wait_p()
    advance(1)
    part = jnp.dot(
        hidden[...].reshape(groups * texts, hidden.shape[2]),
        down[...],
        preferred_element_type=f32,
    )
    share[...] = part.reshape(groups, texts, width)
    pooled[me] = share[me]
    start, wait = along(0, lambda p: share.at[p], lambda p: pooled.at[p], b_send, b_recv)
    start()
    wait()
    terms[col] = pooled[pl.ds(col * split, split)]
    start, wait = along(
        1, lambda p: pooled.at[pl.ds(p * split, split)], lambda p: terms.at[p], c_send, c_recv
    )
    start()
    if parts > 2:
        advance(2)
    wait()
    total = jnp.zeros((texts, embed.shape[1]), f32)
    for i in range(split):
        value = token_mean[:, i * width : (i + 1) * width]
        for p in range(parts):
            value += terms[p, i]
        high = value.astype(bf16)
        low = (value - high.astype(f32)).astype(bf16)
        rows = embed[i * width : (i + 1) * width, :]
        total += jnp.dot(high, rows, preferred_element_type=f32)
        total += jnp.dot(low, rows, preferred_element_type=f32)
    sums[col] = total.astype(bf16)
    start, wait = along(1, lambda p: sums.at[col], lambda p: sums.at[p], d_send, d_recv)
    start()
    wait()
    total = jnp.zeros((texts, embed.shape[1]), f32)
    for p in range(parts):
        total += sums[p].astype(f32)
    fresh[me] = total.astype(bf16)
    start, wait = along(0, lambda p: fresh.at[me], lambda p: fresh.at[p], e_send, e_recv)
    start()
    for far in range(3, parts):
        advance(far)
    finish()
    row = lax.broadcasted_iota(jnp.int32, (texts, count), 1) + me * count
    hits = jnp.concatenate(
        [jnp.where(row == spots[p][:, :1], 1.0, 0.0).astype(bf16) for p in range(groups)], axis=0
    )
    wait()
    for p in range(parts):
        rows = fresh[:, :, p * local : (p + 1) * local].reshape(groups * texts, local)
        added = lax.dot_general(hits, rows, (((0,), (0,)), ((), ())), preferred_element_type=f32)
        states[p] = (nodes[0, p].astype(f32) + added).astype(bf16)

    for layer in range(layers):
        if layer > 0:
            advance, finish = line_copies(
                nodes.at[layer], col, parts, me, cuts, line_send.at[layer], line_recv.at[layer]
            )
            for far in range(parts):
                advance(far)
        block = states if layer == 0 else nodes.at[layer]
        projected = jnp.zeros((count, local), f32)
        for p in range(parts):
            projected += jnp.dot(
                block[p], near_w[p * local : (p + 1) * local, :], preferred_element_type=f32
            )
        here = extended.at[layer]
        here[halo : halo + count, :] = projected.astype(bf16)

        @pl.when(me == 0)
        def _():
            here[0:halo, :] = jnp.zeros((halo, local), bf16)

        @pl.when(me == groups - 1)
        def _():
            here[halo + count :, :] = jnp.zeros((halo, local), bf16)

        def edge(way, incoming):
            step = 1 if way == 0 else -1
            low, high = pl.ds(0, halo), pl.ds(halo + count, halo)
            dst = here.at[low if way == 0 else high]
            src = here.at[pl.ds(count, halo) if way == 0 else pl.ds(halo, halo)]
            to = me + step
            there = (to >= 0) & (to < groups)
            if incoming:
                there = (me - step >= 0) & (me - step < groups)
                src = dst
            return there, pltpu.make_async_remote_copy(
                src_ref=src,
                dst_ref=dst,
                send_sem=halo_send.at[layer, way],
                recv_sem=halo_recv.at[layer, way],
                device_id=(to, col),
                device_id_type=MESH,
            )

        for way in range(2):
            there, copy = edge(way, False)
            pl.when(there)(copy.start)
        if layer > 0:
            finish()
        near = jnp.zeros((count, local), f32)
        for p in range(parts):
            near += jnp.dot(
                block[p], self_w[p * local : (p + 1) * local, :], preferred_element_type=f32
            )
        for way in range(2):
            there, copy = edge(way, True)
            pl.when(there)(copy.wait_recv)
        near += jnp.dot(adjacency[...], here[...], preferred_element_type=f32)
        result = jnp.maximum(near, 0.0).astype(bf16)
        for way in range(2):
            there, copy = edge(way, False)
            pl.when(there)(copy.wait_send)
        if layer < layers - 1:
            nodes[layer + 1, col] = result
        else:
            out[...] = result


def text_and_graph(
    mean, token_mean, down, embed, place, cache, adjacency, self_w, near_w
):
    groups, parts = lax.axis_size("dp"), lax.axis_size("tensor")
    texts, hidden = mean.shape
    width, (count, local) = down.shape[1], cache.shape
    features = embed.shape[1]
    sem = pltpu.SemaphoreType.DMA
    vmem = pl.BlockSpec(memory_space=pltpu.VMEM)
    cuts = 2
    reach = adjacency.shape[1]
    return pl.pallas_call(
        functools.partial(tail_kernel, groups, parts, LAYERS, cuts),
        out_shape=jax.ShapeDtypeStruct((count, local), bf16),
        in_specs=[vmem] * 9,
        out_specs=vmem,
        scratch_shapes=[
            pltpu.VMEM((groups, texts, hidden), bf16),
            pltpu.VMEM((groups,) + place.shape, jnp.int32),
            pltpu.VMEM((groups, texts, width), f32),
            pltpu.VMEM((groups, texts, width), f32),
            pltpu.VMEM((parts, groups // parts, texts, width), f32),
            pltpu.VMEM((parts, texts, features), bf16),
            pltpu.VMEM((groups, texts, features), bf16),
            pltpu.VMEM((parts, count, local), bf16),
            pltpu.VMEM((LAYERS, parts, count, local), bf16),
            pltpu.VMEM((LAYERS, reach, local), bf16),
        ]
        + [sem((groups,))] * 6
        + [sem((parts,))] * 4
        + [sem((groups,))] * 2
        + [sem((LAYERS, 2, parts - 1, cuts))] * 2
        + [sem((LAYERS, 2))] * 2,
        compiler_params=pltpu.CompilerParams(
            collective_id=1, has_side_effects=True, vmem_limit_bytes=40 << 20
        ),
        name="embed_and_layers",
    )(mean, token_mean, down, embed, place, cache, adjacency, self_w, near_w)


def per_device(
    token_states,
    norm_gain,
    gate_weight,
    up_weight,
    down_weight,
    embed_weight,
    text_owner,
    text_row,
    node_cache,
    tile_index,
    tile_live,
    tile_weight,
    self_weight,
    neighbour_weight,
):
    text_count = text_row.shape[0]
    length = token_states.shape[0] // text_count
    node_count = node_cache.shape[0]
    place = jnp.broadcast_to(text_owner * node_count + text_row[:, None], (text_count, 128))
    mean, token_mean, adjacency = pooled_hidden(
        token_states, norm_gain, gate_weight, up_weight, tile_index, tile_live, tile_weight, length
    )
    return text_and_graph(
        mean,
        token_mean,
        down_weight,
        embed_weight,
        place,
        node_cache,
        adjacency,
        self_weight,
        neighbour_weight,
    )


def solution(mesh):
    in_specs = (
        P("dp", "tensor"),
        P(),
        P("dp", "tensor"),
        P("dp", "tensor"),
        P("tensor", "dp"),
        P("tensor", None),
        P("dp", None),
        P("dp"),
        P("dp", "tensor"),
        P("dp", None),
        P("dp", None),
        P("dp", None, None, None),
        P(None, "tensor"),
        P(None, "tensor"),
    )
    out_specs = P("dp", "tensor")
    return jax.shard_map(
        per_device, mesh=mesh, in_specs=in_specs, out_specs=out_specs, check_vma=False
    )
```
